32 devices in a mesh: groups: 2 (over y), ctx: 4 (over z), tp: 2 (over x), dp: 2 (over core).
Axes of the slice: x: 2, y: 2, z: 4, core: 2. Of those that a mesh axis runs over, the one named last changes fastest.
Arguments:
- kv_rows: bfloat16 [32768, 1024], P(('groups', 'ctx', 'dp'), 'tp'), parts along dimension 0, may hold values from -6 to 6
- basis: bfloat16 [1024, 512], P('tp'), may hold values from -0.1875 to 0.1875
- out_weight: bfloat16 [4096, 4096], P('tp'), may hold values from -0.09375 to 0.09375
- queries: bfloat16 [64, 8, 512], P(('groups', 'ctx', 'dp'), 'tp'), parts along dimension 0, may hold values from -80 to 80
- new_kv: bfloat16 [64, 1024], P(('groups', 'ctx', 'dp')), parts along dimension 0, may hold values from -6 to 6
- owner: int32 [64], P('groups'), parts along dimension 0, may hold values from 0 to 7, as said below
- req_start: int32 [16, 32], P(('groups', 'ctx', 'dp')), parts along dimension 0, may hold values from 0 to 2048, as said below
Outputs:
- mixed: bfloat16 [64, 4096], P(('groups', 'ctx', 'dp'), 'tp'), parts along dimension 0
The draws below stay inside these ranges and needn't reach their ends.
There are 2 independent parts, one for each index of `groups`. The reference program is written for one: setup_inputs(seed, part) draws one part's arguments, and reference() takes and returns one part's arrays. A program takes and returns all parts, laid end to end along the dimension named above; an argument that names none is the same for every part. Nothing has to cross between parts.
Inputs may be any that keep to these rules, and one draw needn't show every extreme that they name: Every owner owns exactly 4 requests. `req_start`: along the requests the starts never fall and begin at 0; a request's piece ends where the next begins. One source's pieces of one owner's requests hold at most 768 rows; 1 owners receive exactly 768 rows from every source, the others share the rest nearly evenly.
All inputs are finite; a program needn't handle non-finite values.
Results may differ from the reference program's by a relative error of at most 0.0095.
Values may be sent and summed in bfloat16 or wider, within the bound.
A program may use at most 128 MiB of HBM per device.

```python
import math
import jax
import jax.numpy as jnp
from jax import lax

D = 4096
KVH = 4
HD = 128
QPG = 8
RANK = 512
TOK_DEV = 2048
REQ_OWN = 4
FEAT = 1024
OWNERS = 8
TOKENS = 16384
REQS = 32
SOURCE_TOKEN_MAX = 768
HEAVY = 1


def route_tables(key):
    key_heavy, key_light, key_req, key_cut = jax.random.split(key, 4)
    owner_ids = jnp.arange(OWNERS, dtype=jnp.int32)
    order = jax.random.permutation(key_heavy, OWNERS)
    place = jnp.zeros((OWNERS,), jnp.int32).at[order].set(owner_ids)
    heavy_flags = place < HEAVY
    light_total = TOK_DEV - HEAVY * SOURCE_TOKEN_MAX
    light_count = OWNERS - HEAVY
    count_baseline = light_total // light_count
    surplus_count = light_total % light_count
    jitter = jax.random.randint(key_light, (OWNERS, OWNERS), 0, 1 << 20)
    score = jitter * OWNERS + owner_ids[None, :]
    lower = (score[:, None, :] < score[:, :, None]) & jnp.logical_not(heavy_flags)[None, None, :]
    reduced_rank = jnp.sum(lower.astype(jnp.int32), axis=2)
    added_rank = ((reduced_rank < surplus_count) & jnp.logical_not(heavy_flags)[None, :]).astype(jnp.int32)
    count_table = jnp.where(heavy_flags[None, :], SOURCE_TOKEN_MAX, count_baseline + added_rank).astype(jnp.int32)
    req_order = jax.random.permutation(key_req, REQS)
    owner = (req_order // REQ_OWN).astype(jnp.int32)
    cuts = jax.random.randint(key_cut, (OWNERS, OWNERS, REQ_OWN - 1), 0, count_table[:, :, None] + 1)
    cuts = jnp.sort(cuts, axis=-1)
    edges = jnp.concatenate([jnp.zeros((OWNERS, OWNERS, 1), jnp.int32), cuts.astype(jnp.int32), count_table[:, :, None]], axis=-1)
    portions = edges[:, :, 1:] - edges[:, :, :-1]
    req_ids = jnp.arange(REQS, dtype=jnp.int32)
    earlier = (owner[:, None] == owner[None, :]) & (req_ids[None, :] < req_ids[:, None])
    local_rank = jnp.sum(earlier.astype(jnp.int32), axis=1)
    pieces = portions[:, owner, local_rank]
    starts = jnp.cumsum(pieces, axis=1) - pieces
    return (owner, starts.astype(jnp.int32))


def base_vectors(key):
    return jnp.clip(jax.random.normal(key, (REQS, FEAT), jnp.float32), -6.0, 6.0)


def draw_owner(key, part):
    owner, starts = route_tables(key)
    return owner


def draw_req_start(key, part):
    owner, starts = route_tables(key)
    return starts


def draw_new_kv(key, part):
    return base_vectors(key).astype(jnp.bfloat16)


def draw_queries(key, part):
    key = jax.random.fold_in(key, 7)
    noise = jnp.clip(jax.random.normal(key, (REQS, QPG, KVH * HD), jnp.float32), -6.0, 6.0)
    values = noise
    return values.astype(jnp.bfloat16)


def block_scale(own_key, dims, cuts, smallest, top_value):
    def one(dim, parts):
        steps = jax.random.uniform(jax.random.fold_in(jax.random.fold_in(own_key, 6), dim), (parts,), jnp.float32, smallest / len(cuts), top_value / len(cuts))
        return jnp.repeat(jnp.exp(steps), dims[dim] // parts).reshape((-1,) + (1,) * (len(dims) - dim - 1))

    level = one(*cuts[0])
    for cut in cuts[1:]:
        level = level * one(*cut)
    return level


def centred(stream_key, extent, spread, limit, shards=(), kind=jnp.bfloat16):
    factor_of = block_scale(stream_key, extent, shards, -0.22, 0.18) if shards else 1.0
    values = jax.random.normal(stream_key, extent, jnp.float32) * spread * factor_of
    return jnp.minimum(jnp.maximum(values, -limit), limit).astype(kind)


def setup_inputs(seed: int = 0, part: int = 0) -> dict:
    seeds = jax.random.split(jax.random.key(seed), 8)
    own_keys = jax.random.split(jax.random.fold_in(seeds[7], part), 8)
    kv_rows = centred(own_keys[0], (TOKENS, FEAT), 1.0, 6.0, ((0, 8), (1, 2)))
    basis = centred(seeds[1], (FEAT, RANK), FEAT ** -0.5, 0.1875, ((0, 2),))
    out_weight = centred(seeds[2], (QPG * KVH * HD, D), (QPG * KVH * HD) ** -0.5, 0.09375, ((0, 2),))
    queries = draw_queries(jax.random.fold_in(jax.random.fold_in(seeds[7], part), 71), part)
    new_kv = draw_new_kv(jax.random.fold_in(jax.random.fold_in(seeds[7], part), 71), part)
    owner = draw_owner(jax.random.fold_in(jax.random.fold_in(seeds[7], part), 71), part)
    req_start = draw_req_start(jax.random.fold_in(jax.random.fold_in(seeds[7], part), 71), part)
    return dict(kv_rows=kv_rows, basis=basis, out_weight=out_weight, queries=queries, new_kv=new_kv, owner=owner, req_start=req_start)


def token_slots(owner, req_start):
    row_ids = jnp.arange(TOK_DEV, dtype=jnp.int32)
    inside = (req_start[:, None, :] <= row_ids[None, :, None]).astype(jnp.int32)
    request_of = lax.optimization_barrier(jnp.sum(inside, axis=2)) - 1
    req_ids = jnp.arange(REQS, dtype=jnp.int32)
    earlier = ((owner[:, None] == owner[None, :]) & (req_ids[None, :] < req_ids[:, None])).astype(jnp.int32)
    local_rank = lax.optimization_barrier(jnp.sum(earlier, axis=1))
    slot_of = (owner * REQ_OWN + local_rank).astype(jnp.int32)
    return slot_of[request_of].reshape(TOKENS)

def reference(kv_rows, basis, out_weight, queries, new_kv, owner, req_start):
    coeffs = jnp.dot(kv_rows, basis, preferred_element_type=jnp.float32).astype(jnp.bfloat16)
    rebuilt = jnp.dot(coeffs, basis.T, preferred_element_type=jnp.float32).astype(jnp.bfloat16)
    half_width = KVH * HD
    keys = rebuilt[:, :half_width].astype(jnp.float32).reshape(TOKENS, KVH, HD)
    values = rebuilt[:, half_width:].astype(jnp.float32).reshape(TOKENS, KVH, HD)
    token_slot = token_slots(owner, req_start)
    query_all = queries.astype(jnp.float32).reshape(REQS, QPG, KVH, HD)
    new_keys = new_kv[:, :half_width].astype(jnp.float32).reshape(REQS, KVH, HD)
    new_values = new_kv[:, half_width:].astype(jnp.float32).reshape(REQS, KVH, HD)
    scale = 1.0 / math.sqrt(HD)

    def attend(slot):
        query_one = query_all[slot]
        scores = jnp.einsum('jgd,ngd->jgn', query_one, keys) * scale
        live = (token_slot == slot)[None, None, :]
        scores = jnp.where(live, scores, -1e+30)
        own_score = jnp.einsum('jgd,gd->jg', query_one, new_keys[slot]) * scale
        top = jnp.maximum(lax.optimization_barrier(jnp.max(scores, axis=2)), own_score)
        weights = jnp.where(live, jnp.exp(scores - top[:, :, None]), 0.0)
        own_weight = jnp.exp(own_score - top)
        total = lax.optimization_barrier(jnp.sum(weights, axis=2)) + own_weight
        weights = lax.optimization_barrier((weights / total[:, :, None]).astype(jnp.bfloat16)).astype(jnp.float32)
        own_weight = lax.optimization_barrier((own_weight / total).astype(jnp.bfloat16)).astype(jnp.float32)
        mixed_one = jnp.einsum('jgn,ngd->jgd', weights, values) + own_weight[:, :, None] * new_values[slot][None, :, :]
        return mixed_one.astype(jnp.bfloat16)
    attended = lax.map(attend, jnp.arange(REQS, dtype=jnp.int32))
    attended = attended.reshape(REQS, QPG * KVH * HD)
    return jnp.dot(attended, out_weight, preferred_element_type=jnp.float32).astype(jnp.bfloat16)
```

```python
import math

import jax
import jax.numpy as jnp
from jax import lax
from jax.sharding import PartitionSpec as P

HD = 128


def token_slots(owner, req_start, row_count, slot_own):
    starts = req_start[0]
    req_count = starts.shape[0]
    row_ids = jnp.arange(row_count, dtype=jnp.int32)
    req_ids = jnp.arange(req_count, dtype=jnp.int32)
    inside = (starts[None, :] <= row_ids[:, None]).astype(jnp.int32)
    request_of = jnp.sum(inside, axis=1) - 1
    picked = (request_of[:, None] == req_ids[None, :]).astype(jnp.int32)
    earlier = (owner[:, None] == owner[None, :]) & (req_ids[None, :] < req_ids[:, None])
    slot_of = owner * slot_own + jnp.sum(earlier.astype(jnp.int32), axis=1)
    return jnp.sum(picked * slot_of[None, :], axis=1)


def on_device(kv_rows, basis, out_weight, queries, new_kv, owner, req_start):
    owners = lax.axis_size("ctx") * lax.axis_size("dp")
    rows, feat = kv_rows.shape
    own_slots, local_j, half = queries.shape
    groups = half // HD
    f32, bf16 = jnp.float32, jnp.bfloat16
    scale = 1.0 / math.sqrt(HD)
    whole_basis = lax.all_gather(basis, "tp", axis=0, tiled=True)
    rank = basis.shape[1]
    basis_k = whole_basis[:half].reshape(groups, HD, rank)
    basis_v = whole_basis[half:].reshape(groups, HD, rank)
    q_all = lax.all_gather(queries, ("ctx", "dp"), axis=0, tiled=True)
    q_all = lax.all_gather(q_all, "tp", axis=1, tiled=True)
    slots, heads = q_all.shape[:2]
    q4 = q_all.reshape(slots, heads, groups, HD)
    q_rank = jnp.einsum("rjgd,gdl->grjl", q4, basis_k, preferred_element_type=f32).astype(bf16)
    q_feat = jnp.einsum("grjl,fl->grjf", q_rank, basis, preferred_element_type=f32).astype(bf16)
    slot = token_slots(owner, req_start, rows, own_slots)
    slot_ids = jnp.arange(slots, dtype=jnp.int32)
    live = slot_ids[:, None] == slot[None, :]
    dense = jnp.einsum("grjf,nf->grjn", q_feat, kv_rows, preferred_element_type=f32)
    part = jnp.sum(jnp.where(live[None, :, None, :], dense, 0.0), axis=1)
    score = lax.psum(part, "tp") * scale
    top = jnp.max(jnp.where(live[None, :, None, :], score[:, None], -1e30), axis=3)
    top_tok = jnp.sum(jnp.where(live[None, :, None, :], top[..., None], 0.0), axis=1)
    p = jnp.exp(score - top_tok)
    spread = jnp.where(live[None, :, None, :], p[:, None], 0.0)
    total = jnp.sum(spread, axis=3)
    mixed = jnp.einsum("grjn,nf->grjf", spread.astype(bf16), kv_rows, preferred_element_type=f32)
    mixed = jnp.einsum("grjf,fl->grjl", mixed.astype(bf16), basis, preferred_element_type=f32)
    mixed = jnp.einsum("grjl,gdl->jrgd", mixed.astype(bf16), basis_v, preferred_element_type=f32)
    mixed = lax.psum_scatter(mixed.astype(bf16), "tp", scatter_dimension=0, tiled=True)
    first_j = lax.axis_index("tp") * local_j
    stats = jnp.stack([top, total]).transpose(3, 2, 1, 0)
    stats = lax.dynamic_slice_in_dim(stats, first_j, local_j, axis=0)
    mixed = lax.all_to_all(
        mixed.reshape(local_j, owners, own_slots, groups, HD), ("ctx", "dp"), 1, 1, tiled=True
    ).astype(f32)
    stats = lax.all_to_all(
        stats.reshape(local_j, owners, own_slots, groups, 2), ("ctx", "dp"), 1, 1, tiled=True
    )
    q_own = queries.reshape(own_slots, local_j, groups, HD)
    new_keys = new_kv[:, :half].reshape(own_slots, groups, HD)
    new_values = new_kv[:, half:].reshape(own_slots, groups, HD)
    own = jnp.einsum("rjgd,rgd->jrg", q_own, new_keys, preferred_element_type=f32) * scale
    tops, totals = stats[..., 0], stats[..., 1]
    best = jnp.maximum(jnp.max(tops, axis=1), own)
    lift = jnp.exp(tops - best[:, None])
    own_w = jnp.exp(own - best)
    denom = jnp.sum(lift * totals, axis=1) + own_w
    att = jnp.sum(lift[..., None] * mixed, axis=1)
    att = att + own_w[..., None] * new_values.astype(f32)[None]
    att = (att / denom[..., None]).astype(bf16)
    att = att.transpose(1, 0, 2, 3).reshape(own_slots, local_j * half)
    out = jnp.dot(att, out_weight, preferred_element_type=f32)
    return lax.psum_scatter(out.astype(bf16), "tp", scatter_dimension=1, tiled=True)


def solution(mesh):
    return jax.shard_map(
        on_device,
        mesh=mesh,
        in_specs=(
            P(("groups", "ctx", "dp"), "tp"),
            P("tp", None),
            P("tp", None),
            P(("groups", "ctx", "dp"), "tp", None),
            P(("groups", "ctx", "dp"), None),
            P("groups"),
            P(("groups", "ctx", "dp"), None),
        ),
        out_specs=P(("groups", "ctx", "dp"), "tp"),
        check_vma=False,
    )
```

```python
import math

import jax
import jax.numpy as jnp
from jax import lax
from jax.experimental import pallas as pl
from jax.experimental.pallas import tpu as pltpu
from jax.sharding import PartitionSpec as P

HD = 128


def token_slots(owner, req_start, row_count, slot_own):
    starts = req_start[0]
    req_count = starts.shape[0]
    row_ids = jnp.arange(row_count, dtype=jnp.int32)
    req_ids = jnp.arange(req_count, dtype=jnp.int32)
    inside = (starts[None, :] <= row_ids[:, None]).astype(jnp.int32)
    request_of = jnp.sum(inside, axis=1) - 1
    picked = (request_of[:, None] == req_ids[None, :]).astype(jnp.int32)
    earlier = (owner[:, None] == owner[None, :]) & (req_ids[None, :] < req_ids[:, None])
    slot_of = owner * slot_own + jnp.sum(earlier.astype(jnp.int32), axis=1)
    return jnp.sum(picked * slot_of[None, :], axis=1)


def by_collectives(kv_rows, basis, out_weight, queries, new_kv, owner, req_start):
    owners = lax.axis_size("ctx") * lax.axis_size("dp")
    rows, feat = kv_rows.shape
    own_slots, local_j, half = queries.shape
    groups = half // HD
    f32, bf16 = jnp.float32, jnp.bfloat16
    scale = 1.0 / math.sqrt(HD)
    whole_basis = lax.all_gather(basis, "tp", axis=0, tiled=True)
    rank = basis.shape[1]
    basis_k = whole_basis[:half].reshape(groups, HD, rank)
    basis_v = whole_basis[half:].reshape(groups, HD, rank)
    q_all = lax.all_gather(queries, ("ctx", "dp"), axis=0, tiled=True)
    q_all = lax.all_gather(q_all, "tp", axis=1, tiled=True)
    slots, heads = q_all.shape[:2]
    q4 = q_all.reshape(slots, heads, groups, HD)
    q_rank = jnp.einsum("rjgd,gdl->grjl", q4, basis_k, preferred_element_type=f32).astype(bf16)
    q_feat = jnp.einsum("grjl,fl->grjf", q_rank, basis, preferred_element_type=f32).astype(bf16)
    slot = token_slots(owner, req_start, rows, own_slots)
    slot_ids = jnp.arange(slots, dtype=jnp.int32)
    live = slot_ids[:, None] == slot[None, :]
    dense = jnp.einsum("grjf,nf->grjn", q_feat, kv_rows, preferred_element_type=f32)
    part = jnp.sum(jnp.where(live[None, :, None, :], dense, 0.0), axis=1)
    score = lax.psum(part, "tp") * scale
    top = jnp.max(jnp.where(live[None, :, None, :], score[:, None], -1e30), axis=3)
    top_tok = jnp.sum(jnp.where(live[None, :, None, :], top[..., None], 0.0), axis=1)
    p = jnp.exp(score - top_tok)
    spread = jnp.where(live[None, :, None, :], p[:, None], 0.0)
    total = jnp.sum(spread, axis=3)
    mixed = jnp.einsum("grjn,nf->grjf", spread.astype(bf16), kv_rows, preferred_element_type=f32)
    mixed = jnp.einsum("grjf,fl->grjl", mixed.astype(bf16), basis, preferred_element_type=f32)
    mixed = jnp.einsum("grjl,gdl->jrgd", mixed.astype(bf16), basis_v, preferred_element_type=f32)
    mixed = lax.psum_scatter(mixed.astype(bf16), "tp", scatter_dimension=0, tiled=True)
    first_j = lax.axis_index("tp") * local_j
    stats = jnp.stack([top, total]).transpose(3, 2, 1, 0)
    stats = lax.dynamic_slice_in_dim(stats, first_j, local_j, axis=0)
    mixed = lax.all_to_all(
        mixed.reshape(local_j, owners, own_slots, groups, HD), ("ctx", "dp"), 1, 1, tiled=True
    ).astype(f32)
    stats = lax.all_to_all(
        stats.reshape(local_j, owners, own_slots, groups, 2), ("ctx", "dp"), 1, 1, tiled=True
    )
    q_own = queries.reshape(own_slots, local_j, groups, HD)
    new_keys = new_kv[:, :half].reshape(own_slots, groups, HD)
    new_values = new_kv[:, half:].reshape(own_slots, groups, HD)
    own = jnp.einsum("rjgd,rgd->jrg", q_own, new_keys, preferred_element_type=f32) * scale
    tops, totals = stats[..., 0], stats[..., 1]
    best = jnp.maximum(jnp.max(tops, axis=1), own)
    lift = jnp.exp(tops - best[:, None])
    own_w = jnp.exp(own - best)
    denom = jnp.sum(lift * totals, axis=1) + own_w
    att = jnp.sum(lift[..., None] * mixed, axis=1)
    att = att + own_w[..., None] * new_values.astype(f32)[None]
    att = (att / denom[..., None]).astype(bf16)
    att = att.transpose(1, 0, 2, 3).reshape(own_slots, local_j * half)
    out = jnp.dot(att, out_weight, preferred_element_type=f32)
    return lax.psum_scatter(out.astype(bf16), "tp", scatter_dimension=1, tiled=True)

NT = (((1,), (1,)), ((), ()))
NN = (((1,), (0,)), ((), ()))
LOW = -1e30
CHUNKS = 4


def dot(a, b, dims=NN):
    return lax.dot_general(a, b, dims, preferred_element_type=jnp.float32)


def roll4(x):
    return pltpu.roll(x, 4, 0)


def handoff_kernel(
    owner_ref, start_ref, q_ref, new_ref, basis_ref, kv_hbm, w_hbm, out_ref,
    kv, w, qbuf, bbuf, gram_k, gram_v, qf, slotm_ref, ssend, srecv, sdup, p_scr, tops,
    pblk, asend, arecv, tsend, trecv, x16, osend, orecv,
    loc_sem, q1_sem, qs_sem, qr_sem, b_sem, s_sem, r_sem, as_sem, ar_sem, ts_sem, tr_sem, o_sem,
):
    f32, bf16, i32 = jnp.float32, jnp.bfloat16, jnp.int32
    owners = qbuf.shape[0]
    slots = 4 * owners
    rows = kv.shape[0]
    cn = rows // CHUNKS
    scale = 1.0 / math.sqrt(HD)
    dp, tp = lax.axis_index("dp"), lax.axis_index("tp")
    me = lax.axis_index("ctx") * 2 + dp
    oth = 1 - tp
    half_cols = w.shape[2]

    def at(o, t):
        return {"ctx": o // 2, "dp": lax.rem(o, 2), "tp": t}

    def remote(src, dst, ssem, rsem, o, t):
        return pltpu.make_async_remote_copy(
            src_ref=src, dst_ref=dst, send_sem=ssem, recv_sem=rsem,
            device_id=at(o, t), device_id_type=pl.DeviceIdType.MESH,
        )

    kv_copy = pltpu.make_async_copy(kv_hbm, kv, loc_sem.at[0])
    kv_copy.start()
    w_copies = []
    for h, side in enumerate((oth, tp)):
        cols = pl.ds(pl.multiple_of(side * half_cols, half_cols), half_cols)
        w_copies.append(pltpu.make_async_copy(w_hbm.at[:, cols], w.at[h], loc_sem.at[1 + h]))
        w_copies[-1].start()

    barrier = pltpu.get_barrier_semaphore()

    def greet(i, c):
        o = lax.rem(me + i, owners)
        for t in range(2):
            pl.semaphore_signal(barrier, inc=1, device_id=at(o, t), device_id_type=pl.DeviceIdType.MESH)
        return c

    lax.fori_loop(1, owners, greet, 0)
    pl.semaphore_signal(barrier, inc=1, device_id=at(me, oth), device_id_type=pl.DeviceIdType.MESH)
    pl.semaphore_wait(barrier, 2 * owners - 1)

    q1 = remote(q_ref, qbuf.at[me, tp], q1_sem.at[0], q1_sem.at[1], me, oth)
    q1.start()
    hb = bbuf.shape[2]
    b1 = remote(
        basis_ref.at[pl.ds(pl.multiple_of(dp * hb, hb), hb)], bbuf.at[tp, dp],
        b_sem.at[0], b_sem.at[1], me, oth,
    )
    b1.start()
    qbuf[me, tp] = q_ref[...]
    q1.wait()

    def q_copy(o, src):
        return remote(qbuf.at[me], qbuf.at[src], qs_sem.at[o], qr_sem.at[src], o, tp)

    def q_start(i, c):
        q_copy(lax.rem(me + i, owners), me).start()
        return c

    lax.fori_loop(1, owners, q_start, 0)

    bbuf[tp, 0] = basis_ref[:hb]
    bbuf[tp, 1] = basis_ref[hb:]
    req = owner_ref.shape[1]
    ri = lax.broadcasted_iota(i32, (req, req), 0)
    ci = lax.broadcasted_iota(i32, (req, req), 1)

    def column(row, shift=0):
        return jnp.sum(jnp.where(ci == ri + shift, jnp.broadcast_to(row, (req, req)), 0), axis=1, keepdims=True)

    own_row = owner_ref[...]
    own_col = column(own_row)
    same = (own_row == own_col) & (ci < ri)
    slot_col = own_col * 4 + jnp.sum(jnp.where(same, 1, 0), axis=1, keepdims=True)
    first = column(start_ref[...])
    rc = lax.broadcasted_iota(i32, (req, 1), 0)
    last = column(start_ref[...], 1) + jnp.where(rc == req - 1, rows, 0)
    tok = lax.broadcasted_iota(i32, (req, rows), 1)
    slot = jnp.sum(jnp.where((tok >= first) & (tok < last), slot_col, 0), axis=0, keepdims=True)
    slotm_ref[...] = jnp.broadcast_to(slot, (8, rows)) - lax.broadcasted_iota(i32, (8, rows), 0) // 4

    lane_g = lax.broadcasted_iota(i32, (16, 128), 1) // 32
    row_k = lax.broadcasted_iota(i32, (16, 1), 0) // 4
    fresh = jnp.zeros((16, 1024), f32)
    for k in range(4):
        fresh = jnp.where(row_k == k, new_ref[k : k + 1, :].astype(f32), fresh)
    qk = q_ref[...].astype(f32) * fresh[:, :512]
    own = jnp.zeros((16, 128), f32)
    for g in range(4):
        s = jnp.sum(qk[:, g * HD : (g + 1) * HD], axis=1, keepdims=True) * scale
        own = jnp.where(lane_g == g, s, own)

    b1.wait()
    sib = 2 * lax.axis_index("ctx") + 1 - dp
    b2 = remote(bbuf.at[oth, dp], bbuf.at[oth, dp], b_sem.at[2], b_sem.at[3], sib, tp)
    b2.start()
    b2.wait()
    full_k = bbuf[0].reshape(512, 512)
    full_v = bbuf[1].reshape(512, 512)
    gram_k[...] = dot(full_k, basis_ref[...], NT).astype(bf16)
    gram_v[...] = dot(basis_ref[...], full_v, NT).astype(bf16)

    def q_wait(i, c):
        o = lax.rem(me + i, owners)
        cp = q_copy(o, o)
        cp.wait_recv()
        q_copy(o, me).wait_send()
        return c

    lax.fori_loop(1, owners, q_wait, 0)
    q_rows = qbuf[...].reshape(slots * 8, 512)
    for g in range(4):
        qf[g] = dot(q_rows[:, g * HD : (g + 1) * HD], gram_k[g * HD : (g + 1) * HD, :]).astype(bf16)
    kv_copy.wait()

    low8 = lax.broadcasted_iota(i32, (8, cn), 0) < 4

    def s_copy(c):
        return remote(ssend.at[c], srecv.at[c], s_sem.at[c], r_sem.at[c], me, oth)

    def score_chunk(c, carry):
        span = pl.ds(pl.multiple_of(c * cn, cn), cn)
        kvc = kv[span, :]
        sm = slotm_ref[:, span]
        for g in range(4):
            dense = dot(qf[g], kvc, NT)
            folded = []
            for t in range(2):
                acc = jnp.zeros((8, cn), f32)
                for o in range(owners):
                    for k2 in range(2):
                        r0 = o * 32 + t * 16 + k2 * 8
                        acc = jnp.where(sm == o * 4 + 2 * k2, dense[r0 : r0 + 8], acc)
                folded.append(acc)
            folded = [a + roll4(a) for a in folded]
            ssend[c, g * 8 : (g + 1) * 8, :] = jnp.where(low8, folded[0], folded[1])
        s_copy(c).start()
        return carry

    lax.fori_loop(0, CHUNKS, score_chunk, 0)

    def merge_chunk(c, carry):
        span = pl.ds(pl.multiple_of(c * cn, cn), cn)
        s_copy(c).wait()
        for g in range(4):
            part = (ssend[c, g * 8 : (g + 1) * 8, :] + srecv[c, g * 8 : (g + 1) * 8, :]) * scale
            turned = roll4(part)
            sdup[2 * g, :, span] = jnp.where(low8, part, turned)
            sdup[2 * g + 1, :, span] = jnp.where(low8, turned, part)
        return carry

    lax.fori_loop(0, CHUNKS, merge_chunk, 0)

    def soft(gt, carry):
        s = sdup[gt]
        sm = slotm_ref[...]
        top_tok = jnp.zeros((8, rows), f32)
        for c in range(2 * owners):
            live = sm == 2 * c
            top = jnp.max(jnp.where(live, s, LOW), axis=1, keepdims=True)
            tops[c, gt] = jnp.broadcast_to(top, (8, 128))
            top_tok = jnp.where(live, top, top_tok)
        top_tok = top_tok + roll4(top_tok)
        p_scr[gt] = jnp.exp(s - top_tok)
        return carry

    lax.fori_loop(0, 8, soft, 0)

    def a_copies(o, so):
        return [
            remote(asend.at[o * 2 + t], arecv.at[so * 2 + tp], as_sem.at[o * 2 + t], ar_sem.at[so * 2 + tp], o, t)
            for t in range(2)
        ]

    def t_copy(o, so):
        return remote(tsend.at[o], trecv.at[so], ts_sem.at[o], tr_sem.at[so], o, tp)

    def share(o):
        sm = slotm_ref[...]
        tot = []
        for gt in range(8):
            p = p_scr[gt]
            tiles = [jnp.where(sm == o * 4 + 2 * k2, p, 0.0) for k2 in range(2)]
            both = jnp.concatenate(tiles, axis=0)
            tot.append(jnp.sum(both, axis=1, keepdims=True))
            pblk[gt * 16 : (gt + 1) * 16, :] = both.astype(bf16)
        u = dot(pblk[...], kv[...]).astype(bf16)
        stat = jnp.full((16, 128), LOW, f32)
        for g in range(4):
            a = dot(u[g * 32 : (g + 1) * 32], gram_v[:, g * HD : (g + 1) * HD])
            lse = []
            for t in range(2):
                l = tot[2 * g + t]
                inv = 1.0 / jnp.where(l > 0.0, l, 1.0)
                asend[o * 2 + t, :, g * HD : (g + 1) * HD] = (a[t * 16 : (t + 1) * 16] * inv).astype(bf16)
                top = jnp.concatenate([tops[2 * o, 2 * g + t], tops[2 * o + 1, 2 * g + t]], axis=0)
                lse.append(jnp.where(l > 0.0, top + jnp.log(jnp.where(l > 0.0, l, 1.0)), LOW))
            stat = jnp.where(lane_g == g, jnp.where(tp == 0, lse[0], lse[1]), stat)
        tsend[o] = stat

    def share_send(i, carry):
        o = lax.rem(me + i, owners)
        share(o)
        for cp in a_copies(o, me):
            cp.start()
        t_copy(o, me).start()
        return carry

    lax.fori_loop(1, owners, share_send, 0)
    share(me)
    pair = remote(
        asend.at[me * 2 + oth], arecv.at[me * 2 + tp], as_sem.at[me * 2 + oth], ar_sem.at[me * 2 + tp], me, oth
    )
    pair.start()
    arecv[me * 2 + tp] = asend[me * 2 + tp]
    trecv[me] = tsend[me]

    def share_wait(i, carry):
        o = lax.rem(me + i, owners)
        for cp in a_copies(o, me):
            cp.wait_send()
        t_copy(o, me).wait_send()
        for t in range(2):
            remote(
                asend.at[o * 2 + t], arecv.at[o * 2 + t], as_sem.at[o * 2 + t], ar_sem.at[o * 2 + t], o, t
            ).wait_recv()
        t_copy(o, o).wait_recv()
        return carry

    lax.fori_loop(1, owners, share_wait, 0)
    pair.wait_send()
    remote(
        asend.at[me * 2 + oth], arecv.at[me * 2 + oth], as_sem.at[me * 2 + oth], ar_sem.at[me * 2 + oth], me, oth
    ).wait_recv()

    best = own
    for s in range(owners):
        best = jnp.maximum(best, trecv[s])
    own_w = jnp.exp(own - best)
    denom = own_w
    lifts = []
    for s in range(owners):
        lifts.append(jnp.exp(trecv[s] - best))
        denom = denom + lifts[-1]
    inv = 1.0 / denom
    row_j = lax.rem(lax.broadcasted_iota(i32, (16, 1), 0), 4)
    fold = jnp.where(
        lax.broadcasted_iota(i32, (16, 16), 1) // 4 == lax.rem(lax.broadcasted_iota(i32, (16, 16), 0), 4), 1.0, 0.0
    ).astype(bf16)
    for g in range(4):
        cols = slice(g * HD, (g + 1) * HD)
        att = own_w[:, 32 * g : 32 * g + 1] * fresh[:, 512 + g * HD : 512 + (g + 1) * HD]
        for s in range(owners):
            both = arecv[2 * s, :, cols].astype(f32) + arecv[2 * s + 1, :, cols].astype(f32)
            att = att + lifts[s][:, 32 * g : 32 * g + 1] * both
        att = att * inv[:, 32 * g : 32 * g + 1]
        for j in range(4):
            pick = jnp.where(row_j == j, att, 0.0).astype(bf16)
            x16[:, j * 512 + g * HD : j * 512 + (g + 1) * HD] = dot(fold, pick).astype(bf16)

    o_copy = remote(osend, orecv, o_sem.at[0], o_sem.at[1], me, oth)
    quarter = half_cols // 2
    lowq = lax.broadcasted_iota(i32, (8, 256), 0) < 4
    for h in range(2):
        w_copies[h].wait()

        def column_tile(j, carry, h=h):
            left = pl.ds(pl.multiple_of(j * 256, 256), 256)
            right = pl.ds(pl.multiple_of(quarter + j * 256, 256), 256)
            a = dot(x16[...], w[h, :, left])
            b = dot(x16[...], w[h, :, right])
            picked = jnp.where(lowq, a[:8], b[:8])
            if h == 0:
                osend[:, left] = picked
            else:
                out_ref[:, left] = picked
            return carry

        lax.fori_loop(0, quarter // 256, column_tile, 0)
        if h == 0:
            o_copy.start()
    o_copy.wait()
    out_ref[...] = out_ref[...] + orecv[...]


def fused(kv_rows, basis, out_weight, queries, new_kv, owner, req_start):
    f32, bf16 = jnp.float32, jnp.bfloat16
    owners = lax.axis_size("ctx") * lax.axis_size("dp")
    rows = kv_rows.shape[0]
    slots = owners * 4
    half_cols = out_weight.shape[1] // 2
    dma = pltpu.SemaphoreType.DMA
    vm = pl.BlockSpec(memory_space=pltpu.VMEM)
    hbm = pl.BlockSpec(memory_space=pl.ANY)
    out = pl.pallas_call(
        handoff_kernel,
        out_shape=jax.ShapeDtypeStruct((8, half_cols // 2), f32),
        in_specs=[vm, vm, vm, vm, vm, hbm, hbm],
        out_specs=vm,
        scratch_shapes=[
            pltpu.VMEM((rows, 512), bf16),
            pltpu.VMEM((2, out_weight.shape[0], half_cols), bf16),
            pltpu.VMEM((owners, 2, 16, 512), bf16),
            pltpu.VMEM((2, 2, 256, 512), bf16),
            pltpu.VMEM((512, 512), bf16),
            pltpu.VMEM((512, 512), bf16),
            pltpu.VMEM((4, slots * 8, 512), bf16),
            pltpu.VMEM((8, rows), jnp.int32),
            pltpu.VMEM((CHUNKS, 32, rows // CHUNKS), f32),
            pltpu.VMEM((CHUNKS, 32, rows // CHUNKS), f32),
            pltpu.VMEM((8, 8, rows), f32),
            pltpu.VMEM((8, 8, rows), f32),
            pltpu.VMEM((2 * owners, 8, 8, 128), f32),
            pltpu.VMEM((128, rows), bf16),
            pltpu.VMEM((2 * owners, 16, 512), bf16),
            pltpu.VMEM((2 * owners, 16, 512), bf16),
            pltpu.VMEM((owners, 16, 128), f32),
            pltpu.VMEM((owners, 16, 128), f32),
            pltpu.VMEM((16, out_weight.shape[0]), bf16),
            pltpu.VMEM((8, half_cols // 2), f32),
            pltpu.VMEM((8, half_cols // 2), f32),
            dma((3,)), dma((2,)), dma((owners,)), dma((owners,)), dma((4,)),
            dma((CHUNKS,)), dma((CHUNKS,)),
            dma((2 * owners,)), dma((2 * owners,)), dma((owners,)), dma((owners,)), dma((2,)),
        ],
        compiler_params=pltpu.CompilerParams(
            collective_id=0, has_side_effects=True, vmem_limit_bytes=56 * 1024 * 1024
        ),
    )(
        owner.reshape(1, -1), req_start, queries.reshape(16, 512), new_kv, basis, kv_rows, out_weight,
    )
    return jnp.concatenate([out[:4], out[4:]], axis=1).astype(bf16)


def on_device(kv_rows, basis, out_weight, queries, new_kv, owner, req_start):
    args = (kv_rows, basis, out_weight, queries, new_kv, owner, req_start)
    if queries.shape == (4, 4, 512) and lax.axis_size("tp") == 2 and lax.axis_size("dp") == 2:
        return fused(*args)
    return by_collectives(*args)


def solution(mesh):
    return jax.shard_map(
        on_device,
        mesh=mesh,
        in_specs=(
            P(("groups", "ctx", "dp"), "tp"),
            P("tp", None),
            P("tp", None),
            P(("groups", "ctx", "dp"), "tp", None),
            P(("groups", "ctx", "dp"), None),
            P("groups"),
            P(("groups", "ctx", "dp"), None),
        ),
        out_specs=P(("groups", "ctx", "dp"), "tp"),
        check_vma=False,
    )
```

```python
import math

import jax
import jax.numpy as jnp
from jax import lax
from jax.experimental import pallas as pl
from jax.experimental.pallas import tpu as pltpu
from jax.sharding import PartitionSpec as P

HD = 128


def token_slots(owner, req_start, row_count, slot_own):
    starts = req_start[0]
    req_count = starts.shape[0]
    row_ids = jnp.arange(row_count, dtype=jnp.int32)
    req_ids = jnp.arange(req_count, dtype=jnp.int32)
    inside = (starts[None, :] <= row_ids[:, None]).astype(jnp.int32)
    request_of = jnp.sum(inside, axis=1) - 1
    picked = (request_of[:, None] == req_ids[None, :]).astype(jnp.int32)
    earlier = (owner[:, None] == owner[None, :]) & (req_ids[None, :] < req_ids[:, None])
    slot_of = owner * slot_own + jnp.sum(earlier.astype(jnp.int32), axis=1)
    return jnp.sum(picked * slot_of[None, :], axis=1)


def by_collectives(kv_rows, basis, out_weight, queries, new_kv, owner, req_start):
    owners = lax.axis_size("ctx") * lax.axis_size("dp")
    rows, feat = kv_rows.shape
    own_slots, local_j, half = queries.shape
    groups = half // HD
    f32, bf16 = jnp.float32, jnp.bfloat16
    scale = 1.0 / math.sqrt(HD)
    whole_basis = lax.all_gather(basis, "tp", axis=0, tiled=True)
    rank = basis.shape[1]
    basis_k = whole_basis[:half].reshape(groups, HD, rank)
    basis_v = whole_basis[half:].reshape(groups, HD, rank)
    q_all = lax.all_gather(queries, ("ctx", "dp"), axis=0, tiled=True)
    q_all = lax.all_gather(q_all, "tp", axis=1, tiled=True)
    slots, heads = q_all.shape[:2]
    q4 = q_all.reshape(slots, heads, groups, HD)
    q_rank = jnp.einsum("rjgd,gdl->grjl", q4, basis_k, preferred_element_type=f32).astype(bf16)
    q_feat = jnp.einsum("grjl,fl->grjf", q_rank, basis, preferred_element_type=f32).astype(bf16)
    slot = token_slots(owner, req_start, rows, own_slots)
    slot_ids = jnp.arange(slots, dtype=jnp.int32)
    live = slot_ids[:, None] == slot[None, :]
    dense = jnp.einsum("grjf,nf->grjn", q_feat, kv_rows, preferred_element_type=f32)
    part = jnp.sum(jnp.where(live[None, :, None, :], dense, 0.0), axis=1)
    score = lax.psum(part, "tp") * scale
    top = jnp.max(jnp.where(live[None, :, None, :], score[:, None], -1e30), axis=3)
    top_tok = jnp.sum(jnp.where(live[None, :, None, :], top[..., None], 0.0), axis=1)
    p = jnp.exp(score - top_tok)
    spread = jnp.where(live[None, :, None, :], p[:, None], 0.0)
    total = jnp.sum(spread, axis=3)
    mixed = jnp.einsum("grjn,nf->grjf", spread.astype(bf16), kv_rows, preferred_element_type=f32)
    mixed = jnp.einsum("grjf,fl->grjl", mixed.astype(bf16), basis, preferred_element_type=f32)
    mixed = jnp.einsum("grjl,gdl->jrgd", mixed.astype(bf16), basis_v, preferred_element_type=f32)
    mixed = lax.psum_scatter(mixed.astype(bf16), "tp", scatter_dimension=0, tiled=True)
    first_j = lax.axis_index("tp") * local_j
    stats = jnp.stack([top, total]).transpose(3, 2, 1, 0)
    stats = lax.dynamic_slice_in_dim(stats, first_j, local_j, axis=0)
    mixed = lax.all_to_all(
        mixed.reshape(local_j, owners, own_slots, groups, HD), ("ctx", "dp"), 1, 1, tiled=True
    ).astype(f32)
    stats = lax.all_to_all(
        stats.reshape(local_j, owners, own_slots, groups, 2), ("ctx", "dp"), 1, 1, tiled=True
    )
    q_own = queries.reshape(own_slots, local_j, groups, HD)
    new_keys = new_kv[:, :half].reshape(own_slots, groups, HD)
    new_values = new_kv[:, half:].reshape(own_slots, groups, HD)
    own = jnp.einsum("rjgd,rgd->jrg", q_own, new_keys, preferred_element_type=f32) * scale
    tops, totals = stats[..., 0], stats[..., 1]
    best = jnp.maximum(jnp.max(tops, axis=1), own)
    lift = jnp.exp(tops - best[:, None])
    own_w = jnp.exp(own - best)
    denom = jnp.sum(lift * totals, axis=1) + own_w
    att = jnp.sum(lift[..., None] * mixed, axis=1)
    att = att + own_w[..., None] * new_values.astype(f32)[None]
    att = (att / denom[..., None]).astype(bf16)
    att = att.transpose(1, 0, 2, 3).reshape(own_slots, local_j * half)
    out = jnp.dot(att, out_weight, preferred_element_type=f32)
    return lax.psum_scatter(out.astype(bf16), "tp", scatter_dimension=1, tiled=True)

NT = (((1,), (1,)), ((), ()))
NN = (((1,), (0,)), ((), ()))
LOW = -1e30
CHUNKS = 4


def dot(a, b, dims=NN):
    return lax.dot_general(a, b, dims, preferred_element_type=jnp.float32)


def roll4(x):
    return pltpu.roll(x, 4, 0)


def handoff_kernel(
    owner_ref, start_ref, q3_ref, new_ref, basis_ref, kv_hbm, w_hbm, out_ref,
    kv, w, q_ref, qbuf, bbuf, gram_k, gram_v, qf, slotm_ref, mine, ssend, srecv, sdup, p_scr, tops,
    pblk, asend, arecv, tsend, trecv, x16, osend, orecv, outf,
    loc_sem, q1_sem, qs_sem, qr_sem, b_sem, s_sem, r_sem, as_sem, ar_sem, ts_sem, tr_sem, o_sem,
):
    f32, bf16, i32 = jnp.float32, jnp.bfloat16, jnp.int32
    owners = qbuf.shape[0]
    slots = 4 * owners
    rows = kv.shape[0]
    cn = rows // CHUNKS
    scale = 1.0 / math.sqrt(HD)
    dp, tp = lax.axis_index("dp"), lax.axis_index("tp")
    me = lax.axis_index("ctx") * 2 + dp
    oth = 1 - tp
    half_cols = w.shape[2]

    def at(o, t):
        return {"ctx": o // 2, "dp": lax.rem(o, 2), "tp": t}

    def remote(src, dst, ssem, rsem, o, t):
        return pltpu.make_async_remote_copy(
            src_ref=src, dst_ref=dst, send_sem=ssem, recv_sem=rsem,
            device_id=at(o, t), device_id_type=pl.DeviceIdType.MESH,
        )

    kv_copy = pltpu.make_async_copy(kv_hbm, kv, loc_sem.at[0])
    kv_copy.start()
    w_copies = []
    for h, side in enumerate((oth, tp)):
        cols = pl.ds(pl.multiple_of(side * half_cols, half_cols), half_cols)
        w_copies.append(pltpu.make_async_copy(w_hbm.at[:, cols], w.at[h], loc_sem.at[1 + h]))
        w_copies[-1].start()

    q_ref[...] = jnp.concatenate([q3_ref[k].astype(f32) for k in range(4)], axis=0).astype(bf16)
    barrier = pltpu.get_barrier_semaphore()

    def greet(i, c):
        o = lax.rem(me + i, owners)
        for t in range(2):
            pl.semaphore_signal(barrier, inc=1, device_id=at(o, t), device_id_type=pl.DeviceIdType.MESH)
        return c

    lax.fori_loop(1, owners, greet, 0)
    pl.semaphore_signal(barrier, inc=1, device_id=at(me, oth), device_id_type=pl.DeviceIdType.MESH)
    pl.semaphore_wait(barrier, 2 * owners - 1)

    q1 = remote(q_ref, qbuf.at[me, tp], q1_sem.at[0], q1_sem.at[1], me, oth)
    q1.start()
    hb = bbuf.shape[2]
    b1 = remote(
        basis_ref.at[pl.ds(pl.multiple_of(dp * hb, hb), hb)], bbuf.at[tp, dp],
        b_sem.at[0], b_sem.at[1], me, oth,
    )
    b1.start()
    qbuf[me, tp] = q_ref[...]
    q1.wait()

    def q_copy(o, src):
        return remote(qbuf.at[me], qbuf.at[src], qs_sem.at[o], qr_sem.at[src], o, tp)

    def q_start(i, c):
        q_copy(lax.rem(me + i, owners), me).start()
        return c

    lax.fori_loop(1, owners, q_start, 0)

    bbuf[tp, 0] = basis_ref[:hb]
    bbuf[tp, 1] = basis_ref[hb:]
    req = owner_ref.shape[1]
    ri = lax.broadcasted_iota(i32, (req, req), 0)
    ci = lax.broadcasted_iota(i32, (req, req), 1)

    def column(row, shift=0):
        return jnp.sum(jnp.where(ci == ri + shift, jnp.broadcast_to(row, (req, req)), 0), axis=1, keepdims=True)

    own_row = owner_ref[...]
    own_col = column(own_row)
    same = (own_row == own_col) & (ci < ri)
    slot_col = own_col * 4 + jnp.sum(jnp.where(same, 1, 0), axis=1, keepdims=True)
    first = column(start_ref[...])
    rc = lax.broadcasted_iota(i32, (req, 1), 0)
    last = column(start_ref[...], 1) + jnp.where(rc == req - 1, rows, 0)
    tok = lax.broadcasted_iota(i32, (req, rows), 1)
    slot = jnp.sum(jnp.where((tok >= first) & (tok < last), slot_col, 0), axis=0, keepdims=True)
    slotm_ref[...] = jnp.broadcast_to(slot, (8, rows)) - lax.broadcasted_iota(i32, (8, rows), 0) // 4

    low_lane = lax.rem(lax.broadcasted_iota(i32, (8, 128), 1), 32) < 16
    lane_g = lax.broadcasted_iota(i32, (16, 128), 1) // 32
    row_k = lax.broadcasted_iota(i32, (16, 1), 0) // 4
    fresh = jnp.zeros((16, 1024), f32)
    for k in range(4):
        fresh = jnp.where(row_k == k, new_ref[k : k + 1, :].astype(f32), fresh)
    qk = q_ref[...].astype(f32) * fresh[:, :512]
    own = jnp.zeros((16, 128), f32)
    for g in range(4):
        s = jnp.sum(qk[:, g * HD : (g + 1) * HD], axis=1, keepdims=True) * scale
        own = jnp.where(lane_g == g, s, own)

    b1.wait()
    sib = 2 * lax.axis_index("ctx") + 1 - dp
    b2 = remote(bbuf.at[oth, dp], bbuf.at[oth, dp], b_sem.at[2], b_sem.at[3], sib, tp)
    b2.start()
    b2.wait()
    full_k = bbuf[0].reshape(512, 512)
    full_v = bbuf[1].reshape(512, 512)
    gram_k[...] = dot(full_k, basis_ref[...], NT).astype(bf16)
    gram_v[...] = dot(basis_ref[...], full_v, NT).astype(bf16)

    def q_wait(i, c):
        o = lax.rem(me + i, owners)
        cp = q_copy(o, o)
        cp.wait_recv()
        q_copy(o, me).wait_send()
        return c

    lax.fori_loop(1, owners, q_wait, 0)
    q_rows = qbuf[...].reshape(slots * 8, 512)
    for g in range(4):
        qf[g] = dot(q_rows[:, g * HD : (g + 1) * HD], gram_k[g * HD : (g + 1) * HD, :]).astype(bf16)
    kv_copy.wait()

    low8 = lax.broadcasted_iota(i32, (8, cn), 0) < 4

    def s_copy(c):
        return remote(ssend.at[c], srecv.at[c], s_sem.at[c], r_sem.at[c], me, oth)

    def score_chunk(c, carry):
        span = pl.ds(pl.multiple_of(c * cn, cn), cn)
        kvc = kv[span, :]
        sm = slotm_ref[:, span]
        parts = []
        for g in range(4):
            dense = dot(qf[g], kvc, NT)
            folded = []
            for t in range(2):
                acc = jnp.zeros((8, cn), f32)
                for o in range(owners):
                    for k2 in range(2):
                        r0 = o * 32 + t * 16 + k2 * 8
                        acc = jnp.where(sm == o * 4 + 2 * k2, dense[r0 : r0 + 8], acc)
                folded.append(acc)
            folded = [a + roll4(a) for a in folded]
            parts.append(jnp.where(low8, folded[0], folded[1]))
        parts = jnp.concatenate(parts, axis=0)
        mine[c] = parts
        ssend[c] = parts.astype(bf16)
        s_copy(c).start()
        return carry

    lax.fori_loop(0, CHUNKS, score_chunk, 0)

    def merge_chunk(c, carry):
        span = pl.ds(pl.multiple_of(c * cn, cn), cn)
        s_copy(c).wait()
        both = (mine[c] + srecv[c].astype(f32)) * scale
        for g in range(4):
            part = both[g * 8 : (g + 1) * 8]
            turned = roll4(part)
            sdup[2 * g, :, span] = jnp.where(low8, part, turned)
            sdup[2 * g + 1, :, span] = jnp.where(low8, turned, part)
        return carry

    lax.fori_loop(0, CHUNKS, merge_chunk, 0)

    def soft(gt, carry):
        s = sdup[gt]
        sm = slotm_ref[...]
        top_tok = jnp.zeros((8, rows), f32)
        for c in range(2 * owners):
            live = sm == 2 * c
            top = jnp.max(jnp.where(live, s, LOW), axis=1, keepdims=True)
            tops[c, gt] = jnp.broadcast_to(top, (8, 128))
            top_tok = jnp.where(live, top, top_tok)
        top_tok = top_tok + roll4(top_tok)
        p_scr[gt] = jnp.exp(s - top_tok)
        return carry

    lax.fori_loop(0, 8, soft, 0)

    def a_copies(o, so):
        return [
            remote(asend.at[o * 2 + t], arecv.at[so * 2 + tp], as_sem.at[o * 2 + t], ar_sem.at[so * 2 + tp], o, t)
            for t in range(2)
        ]

    def t_copy(o, so):
        return remote(tsend.at[o], trecv.at[so], ts_sem.at[o], tr_sem.at[so], o, tp)

    def share(ctx):
        sm = slotm_ref[...]
        tot = []
        for d in range(2):
            for gt in range(8):
                p = p_scr[gt]
                tiles = [jnp.where(sm == ctx * 8 + d * 4 + 2 * k2, p, 0.0) for k2 in range(2)]
                both = jnp.concatenate(tiles, axis=0)
                tot.append(jnp.sum(both, axis=1, keepdims=True))
                r0 = d * 128 + gt * 16
                pblk[r0 : r0 + 16, :] = both.astype(bf16)
        u = dot(pblk[...], kv[...]).astype(bf16)
        stats = [jnp.full((16, 128), LOW, f32) for _ in range(2)]
        for g in range(4):
            rows_g = jnp.concatenate([u[d * 128 + g * 32 : d * 128 + (g + 1) * 32] for d in range(2)], axis=0)
            a = dot(rows_g, gram_v[:, g * HD : (g + 1) * HD])
            for d in range(2):
                o = ctx * 2 + d
                lse = []
                for t in range(2):
                    l = tot[d * 8 + 2 * g + t]
                    inv = 1.0 / jnp.where(l > 0.0, l, 1.0)
                    r0 = d * 32 + t * 16
                    asend[o * 2 + t, :, g * HD : (g + 1) * HD] = (a[r0 : r0 + 16] * inv).astype(bf16)
                    top = jnp.concatenate([tops[2 * o, 2 * g + t], tops[2 * o + 1, 2 * g + t]], axis=0)
                    lse.append(jnp.where(l > 0.0, top + jnp.log(jnp.where(l > 0.0, l, 1.0)), LOW))
                stats[d] = jnp.where(lane_g == g, jnp.where(tp == 0, lse[0], lse[1]), stats[d])
        for d in range(2):
            tsend[ctx * 2 + d] = jnp.where(low_lane, stats[d][:8], stats[d][8:])

    my_ctx = lax.axis_index("ctx")

    def send_all(o):
        for cp in a_copies(o, me):
            cp.start()
        t_copy(o, me).start()

    def share_send(i, carry):
        c = lax.rem(my_ctx + i, owners // 2)
        share(c)
        for d in range(2):
            send_all(c * 2 + d)
        return carry

    lax.fori_loop(1, owners // 2, share_send, 0)
    share(my_ctx)
    send_all(sib)
    pair = remote(
        asend.at[me * 2 + oth], arecv.at[me * 2 + tp], as_sem.at[me * 2 + oth], ar_sem.at[me * 2 + tp], me, oth
    )
    pair.start()
    arecv[me * 2 + tp] = asend[me * 2 + tp]
    trecv[me] = tsend[me]

    def share_wait(i, carry):
        o = lax.rem(me + i, owners)
        for cp in a_copies(o, me):
            cp.wait_send()
        t_copy(o, me).wait_send()
        for t in range(2):
            remote(
                asend.at[o * 2 + t], arecv.at[o * 2 + t], as_sem.at[o * 2 + t], ar_sem.at[o * 2 + t], o, t
            ).wait_recv()
        t_copy(o, o).wait_recv()
        return carry

    lax.fori_loop(1, owners, share_wait, 0)
    pair.wait_send()
    remote(
        asend.at[me * 2 + oth], arecv.at[me * 2 + oth], as_sem.at[me * 2 + oth], ar_sem.at[me * 2 + oth], me, oth
    ).wait_recv()

    own = jnp.where(low_lane, own[:8], own[8:])
    best = own
    for s in range(owners):
        best = jnp.maximum(best, trecv[s])
    own_w = jnp.exp(own - best)
    denom = own_w
    lifts = []
    for s in range(owners):
        lifts.append(jnp.exp(trecv[s] - best))
        denom = denom + lifts[-1]
    inv = 1.0 / denom

    def spread(x, g):
        return jnp.concatenate([x[:, 32 * g : 32 * g + 1], x[:, 32 * g + 16 : 32 * g + 17]], axis=0)

    row_j = lax.rem(lax.broadcasted_iota(i32, (16, 1), 0), 4)
    fold = jnp.where(
        lax.broadcasted_iota(i32, (16, 16), 1) // 4 == lax.rem(lax.broadcasted_iota(i32, (16, 16), 0), 4), 1.0, 0.0
    ).astype(bf16)
    for g in range(4):
        cols = slice(g * HD, (g + 1) * HD)
        att = spread(own_w, g) * fresh[:, 512 + g * HD : 512 + (g + 1) * HD]
        for s in range(owners):
            both = arecv[2 * s, :, cols].astype(f32) + arecv[2 * s + 1, :, cols].astype(f32)
            att = att + spread(lifts[s], g) * both
        att = att * spread(inv, g)
        for j in range(4):
            pick = jnp.where(row_j == j, att, 0.0).astype(bf16)
            x16[:, j * 512 + g * HD : j * 512 + (g + 1) * HD] = dot(fold, pick).astype(bf16)

    o_copy = remote(osend, orecv, o_sem.at[0], o_sem.at[1], me, oth)
    quarter = half_cols // 2
    lowq = lax.broadcasted_iota(i32, (8, 256), 0) < 4
    for h in range(2):
        w_copies[h].wait()

        def column_tile(j, carry, h=h):
            left = pl.ds(pl.multiple_of(j * 256, 256), 256)
            right = pl.ds(pl.multiple_of(quarter + j * 256, 256), 256)
            a = dot(x16[...], w[h, :, left])
            b = dot(x16[...], w[h, :, right])
            picked = jnp.where(lowq, a[:8], b[:8])
            if h == 0:
                osend[:, left] = picked
            else:
                outf[:, left] = picked
            return carry

        lax.fori_loop(0, quarter // 256, column_tile, 0)
        if h == 0:
            o_copy.start()
    o_copy.wait()
    total = outf[...] + orecv[...]
    out_ref[:, :quarter] = total[:4].astype(bf16)
    out_ref[:, quarter:] = roll4(total)[:4].astype(bf16)


def fused(kv_rows, basis, out_weight, queries, new_kv, owner, req_start):
    f32, bf16 = jnp.float32, jnp.bfloat16
    owners = lax.axis_size("ctx") * lax.axis_size("dp")
    rows = kv_rows.shape[0]
    slots = owners * 4
    half_cols = out_weight.shape[1] // 2
    dma = pltpu.SemaphoreType.DMA
    vm = pl.BlockSpec(memory_space=pltpu.VMEM)
    hbm = pl.BlockSpec(memory_space=pl.ANY)
    out = pl.pallas_call(
        handoff_kernel,
        out_shape=jax.ShapeDtypeStruct((4, half_cols), bf16),
        in_specs=[vm, vm, vm, vm, vm, hbm, hbm],
        out_specs=vm,
        scratch_shapes=[
            pltpu.VMEM((rows, 512), bf16),
            pltpu.VMEM((2, out_weight.shape[0], half_cols), bf16),
            pltpu.VMEM((16, 512), bf16),
            pltpu.VMEM((owners, 2, 16, 512), bf16),
            pltpu.VMEM((2, 2, 256, 512), bf16),
            pltpu.VMEM((512, 512), bf16),
            pltpu.VMEM((512, 512), bf16),
            pltpu.VMEM((4, slots * 8, 512), bf16),
            pltpu.VMEM((8, rows), jnp.int32),
            pltpu.VMEM((CHUNKS, 32, rows // CHUNKS), f32),
            pltpu.VMEM((CHUNKS, 32, rows // CHUNKS), bf16),
            pltpu.VMEM((CHUNKS, 32, rows // CHUNKS), bf16),
            pltpu.VMEM((8, 8, rows), f32),
            pltpu.VMEM((8, 8, rows), f32),
            pltpu.VMEM((2 * owners, 8, 8, 128), f32),
            pltpu.VMEM((256, rows), bf16),
            pltpu.VMEM((2 * owners, 16, 512), bf16),
            pltpu.VMEM((2 * owners, 16, 512), bf16),
            pltpu.VMEM((owners, 8, 128), f32),
            pltpu.VMEM((owners, 8, 128), f32),
            pltpu.VMEM((16, out_weight.shape[0]), bf16),
            pltpu.VMEM((8, half_cols // 2), f32),
            pltpu.VMEM((8, half_cols // 2), f32),
            pltpu.VMEM((8, half_cols // 2), f32),
            dma((3,)), dma((2,)), dma((owners,)), dma((owners,)), dma((4,)),
            dma((CHUNKS,)), dma((CHUNKS,)),
            dma((2 * owners,)), dma((2 * owners,)), dma((owners,)), dma((owners,)), dma((2,)),
        ],
        compiler_params=pltpu.CompilerParams(
            collective_id=0, has_side_effects=True, vmem_limit_bytes=56 * 1024 * 1024
        ),
    )(
        owner.reshape(1, -1), req_start, queries, new_kv, basis, kv_rows, out_weight,
    )
    return out


def on_device(kv_rows, basis, out_weight, queries, new_kv, owner, req_start):
    args = (kv_rows, basis, out_weight, queries, new_kv, owner, req_start)
    if queries.shape == (4, 4, 512) and lax.axis_size("tp") == 2 and lax.axis_size("dp") == 2:
        return fused(*args)
    return by_collectives(*args)


def solution(mesh):
    return jax.shard_map(
        on_device,
        mesh=mesh,
        in_specs=(
            P(("groups", "ctx", "dp"), "tp"),
            P("tp", None),
            P("tp", None),
            P(("groups", "ctx", "dp"), "tp", None),
            P(("groups", "ctx", "dp"), None),
            P("groups"),
            P(("groups", "ctx", "dp"), None),
        ),
        out_specs=P(("groups", "ctx", "dp"), "tp"),
        check_vma=False,
    )
```

```python
import math

import jax
import jax.numpy as jnp
from jax import lax
from jax.experimental import pallas as pl
from jax.experimental.pallas import tpu as pltpu
from jax.sharding import PartitionSpec as P

HD = 128


def token_slots(owner, req_start, row_count, slot_own):
    starts = req_start[0]
    req_count = starts.shape[0]
    row_ids = jnp.arange(row_count, dtype=jnp.int32)
    req_ids = jnp.arange(req_count, dtype=jnp.int32)
    inside = (starts[None, :] <= row_ids[:, None]).astype(jnp.int32)
    request_of = jnp.sum(inside, axis=1) - 1
    picked = (request_of[:, None] == req_ids[None, :]).astype(jnp.int32)
    earlier = (owner[:, None] == owner[None, :]) & (req_ids[None, :] < req_ids[:, None])
    slot_of = owner * slot_own + jnp.sum(earlier.astype(jnp.int32), axis=1)
    return jnp.sum(picked * slot_of[None, :], axis=1)


def by_collectives(kv_rows, basis, out_weight, queries, new_kv, owner, req_start):
    owners = lax.axis_size("ctx") * lax.axis_size("dp")
    rows, feat = kv_rows.shape
    own_slots, local_j, half = queries.shape
    groups = half // HD
    f32, bf16 = jnp.float32, jnp.bfloat16
    scale = 1.0 / math.sqrt(HD)
    whole_basis = lax.all_gather(basis, "tp", axis=0, tiled=True)
    rank = basis.shape[1]
    basis_k = whole_basis[:half].reshape(groups, HD, rank)
    basis_v = whole_basis[half:].reshape(groups, HD, rank)
    q_all = lax.all_gather(queries, ("ctx", "dp"), axis=0, tiled=True)
    q_all = lax.all_gather(q_all, "tp", axis=1, tiled=True)
    slots, heads = q_all.shape[:2]
    q4 = q_all.reshape(slots, heads, groups, HD)
    q_rank = jnp.einsum("rjgd,gdl->grjl", q4, basis_k, preferred_element_type=f32).astype(bf16)
    q_feat = jnp.einsum("grjl,fl->grjf", q_rank, basis, preferred_element_type=f32).astype(bf16)
    slot = token_slots(owner, req_start, rows, own_slots)
    slot_ids = jnp.arange(slots, dtype=jnp.int32)
    live = slot_ids[:, None] == slot[None, :]
    dense = jnp.einsum("grjf,nf->grjn", q_feat, kv_rows, preferred_element_type=f32)
    part = jnp.sum(jnp.where(live[None, :, None, :], dense, 0.0), axis=1)
    score = lax.psum(part, "tp") * scale
    top = jnp.max(jnp.where(live[None, :, None, :], score[:, None], -1e30), axis=3)
    top_tok = jnp.sum(jnp.where(live[None, :, None, :], top[..., None], 0.0), axis=1)
    p = jnp.exp(score - top_tok)
    spread = jnp.where(live[None, :, None, :], p[:, None], 0.0)
    total = jnp.sum(spread, axis=3)
    mixed = jnp.einsum("grjn,nf->grjf", spread.astype(bf16), kv_rows, preferred_element_type=f32)
    mixed = jnp.einsum("grjf,fl->grjl", mixed.astype(bf16), basis, preferred_element_type=f32)
    mixed = jnp.einsum("grjl,gdl->jrgd", mixed.astype(bf16), basis_v, preferred_element_type=f32)
    mixed = lax.psum_scatter(mixed.astype(bf16), "tp", scatter_dimension=0, tiled=True)
    first_j = lax.axis_index("tp") * local_j
    stats = jnp.stack([top, total]).transpose(3, 2, 1, 0)
    stats = lax.dynamic_slice_in_dim(stats, first_j, local_j, axis=0)
    mixed = lax.all_to_all(
        mixed.reshape(local_j, owners, own_slots, groups, HD), ("ctx", "dp"), 1, 1, tiled=True
    ).astype(f32)
    stats = lax.all_to_all(
        stats.reshape(local_j, owners, own_slots, groups, 2), ("ctx", "dp"), 1, 1, tiled=True
    )
    q_own = queries.reshape(own_slots, local_j, groups, HD)
    new_keys = new_kv[:, :half].reshape(own_slots, groups, HD)
    new_values = new_kv[:, half:].reshape(own_slots, groups, HD)
    own = jnp.einsum("rjgd,rgd->jrg", q_own, new_keys, preferred_element_type=f32) * scale
    tops, totals = stats[..., 0], stats[..., 1]
    best = jnp.maximum(jnp.max(tops, axis=1), own)
    lift = jnp.exp(tops - best[:, None])
    own_w = jnp.exp(own - best)
    denom = jnp.sum(lift * totals, axis=1) + own_w
    att = jnp.sum(lift[..., None] * mixed, axis=1)
    att = att + own_w[..., None] * new_values.astype(f32)[None]
    att = (att / denom[..., None]).astype(bf16)
    att = att.transpose(1, 0, 2, 3).reshape(own_slots, local_j * half)
    out = jnp.dot(att, out_weight, preferred_element_type=f32)
    return lax.psum_scatter(out.astype(bf16), "tp", scatter_dimension=1, tiled=True)

NT = (((1,), (1,)), ((), ()))
NN = (((1,), (0,)), ((), ()))
LOW = -1e30
CHUNKS = 4


def dot(a, b, dims=NN):
    return lax.dot_general(a, b, dims, preferred_element_type=jnp.float32)


def roll4(x):
    return pltpu.roll(x, 4, 0)


def handoff_kernel(
    owner_ref, start_ref, q3_ref, new_ref, basis_ref, kv_hbm, w_hbm, out_ref,
    kv, w, q_ref, qbuf, bbuf, proj, slotm_ref, mine, ssend, srecv, p_scr, tops,
    pblk, asend, arecv, tsend, trecv, x16, osend, orecv, outf,
    loc_sem, q1_sem, qs_sem, qr_sem, b_sem, s_sem, r_sem, as_sem, ar_sem, ts_sem, tr_sem, o_sem,
):
    f32, bf16, i32 = jnp.float32, jnp.bfloat16, jnp.int32
    owners = qbuf.shape[0]
    slots = 4 * owners
    rows = kv.shape[0]
    cn = rows // CHUNKS
    scale = 1.0 / math.sqrt(HD)
    dp, tp = lax.axis_index("dp"), lax.axis_index("tp")
    me = lax.axis_index("ctx") * 2 + dp
    oth = 1 - tp
    half_cols = w.shape[2]

    def at(o, t):
        return {"ctx": o // 2, "dp": lax.rem(o, 2), "tp": t}

    def remote(src, dst, ssem, rsem, o, t):
        return pltpu.make_async_remote_copy(
            src_ref=src, dst_ref=dst, send_sem=ssem, recv_sem=rsem,
            device_id=at(o, t), device_id_type=pl.DeviceIdType.MESH,
        )

    kv_copy = pltpu.make_async_copy(kv_hbm, kv, loc_sem.at[0])
    kv_copy.start()
    w_copies = []
    for h, side in enumerate((oth, tp)):
        cols = pl.ds(pl.multiple_of(side * half_cols, half_cols), half_cols)
        w_copies.append(pltpu.make_async_copy(w_hbm.at[:, cols], w.at[h], loc_sem.at[1 + h]))
        w_copies[-1].start()

    q_ref[...] = jnp.concatenate([q3_ref[k].astype(f32) for k in range(4)], axis=0).astype(bf16)
    barrier = pltpu.get_barrier_semaphore()

    def greet(i, c):
        o = lax.rem(me + i, owners)
        for t in range(2):
            pl.semaphore_signal(barrier, inc=1, device_id=at(o, t), device_id_type=pl.DeviceIdType.MESH)
        return c

    lax.fori_loop(1, owners, greet, 0)
    pl.semaphore_signal(barrier, inc=1, device_id=at(me, oth), device_id_type=pl.DeviceIdType.MESH)
    pl.semaphore_wait(barrier, 2 * owners - 1)

    q1 = remote(q_ref, qbuf.at[me, tp], q1_sem.at[0], q1_sem.at[1], me, oth)
    q1.start()
    sib = 2 * lax.axis_index("ctx") + 1 - dp
    hb = bbuf.shape[3]

    def b_first(g):
        return remote(
            basis_ref.at[pl.ds(pl.multiple_of(g * HD + dp * hb, hb), hb)], bbuf.at[tp, g, dp],
            b_sem.at[g], b_sem.at[4 + g], me, oth,
        )

    def b_second(g):
        return remote(bbuf.at[oth, g, dp], bbuf.at[oth, g, dp], b_sem.at[8 + g], b_sem.at[12 + g], sib, tp)

    for g in range(4):
        b_first(g).start()
    qbuf[me, tp] = q_ref[...]
    q1.wait()

    def q_copy(o, src):
        return remote(qbuf.at[me], qbuf.at[src], qs_sem.at[o], qr_sem.at[src], o, tp)

    def q_start(i, c):
        q_copy(lax.rem(me + i, owners), me).start()
        return c

    lax.fori_loop(1, owners, q_start, 0)

    for g in range(4):
        for d in range(2):
            r0 = g * HD + d * hb
            bbuf[tp, g, d] = basis_ref[r0 : r0 + hb]
    req = owner_ref.shape[1]
    ri = lax.broadcasted_iota(i32, (req, req), 0)
    ci = lax.broadcasted_iota(i32, (req, req), 1)

    def column(row, shift=0):
        return jnp.sum(jnp.where(ci == ri + shift, jnp.broadcast_to(row, (req, req)), 0), axis=1, keepdims=True)

    own_row = owner_ref[...]
    own_col = column(own_row)
    same = (own_row == own_col) & (ci < ri)
    slot_col = own_col * 4 + jnp.sum(jnp.where(same, 1, 0), axis=1, keepdims=True)
    first = column(start_ref[...])
    rc = lax.broadcasted_iota(i32, (req, 1), 0)
    last = column(start_ref[...], 1) + jnp.where(rc == req - 1, rows, 0)
    tok = lax.broadcasted_iota(i32, (req, rows), 1)
    slot = jnp.sum(jnp.where((tok >= first) & (tok < last), slot_col, 0), axis=0, keepdims=True)
    slotm_ref[...] = jnp.broadcast_to(slot, (8, rows)) - lax.broadcasted_iota(i32, (8, rows), 0) // 4

    low_lane = lax.rem(lax.broadcasted_iota(i32, (8, 128), 1), 32) < 16
    lane_g = lax.broadcasted_iota(i32, (16, 128), 1) // 32
    row_k = lax.broadcasted_iota(i32, (16, 1), 0) // 4
    fresh = jnp.zeros((16, 1024), f32)
    for k in range(4):
        fresh = jnp.where(row_k == k, new_ref[k : k + 1, :].astype(f32), fresh)
    qk = q_ref[...].astype(f32) * fresh[:, :512]
    own = jnp.zeros((16, 128), f32)
    for g in range(4):
        s = jnp.sum(qk[:, g * HD : (g + 1) * HD], axis=1, keepdims=True) * scale
        own = jnp.where(lane_g == g, s, own)

    kv_copy.wait()

    def project(c, carry):
        span = pl.ds(pl.multiple_of(c * cn, cn), cn)
        proj[span, :] = dot(kv[span, :], basis_ref[...]).astype(bf16)
        return carry

    lax.fori_loop(0, CHUNKS, project, 0)

    def q_wait(i, c):
        o = lax.rem(me + i, owners)
        cp = q_copy(o, o)
        cp.wait_recv()
        q_copy(o, me).wait_send()
        return c

    lax.fori_loop(1, owners, q_wait, 0)
    q_rows = qbuf[...].reshape(slots * 8, 512)
    low8 = lax.broadcasted_iota(i32, (8, cn), 0) < 4
    half_rows = rows // 2

    def s_copy(g):
        return remote(ssend.at[g], srecv.at[g], s_sem.at[g], r_sem.at[g], me, oth)

    def scores(g):
        b_first(g).wait()
        b_second(g).start()
        b_second(g).wait()
        qg = dot(q_rows[:, g * HD : (g + 1) * HD], bbuf[0, g].reshape(HD, 512)).astype(bf16)

        def score_chunk(c, carry):
            span = pl.ds(pl.multiple_of(c * cn, cn), cn)
            sm = slotm_ref[:, span]
            dense = dot(qg, proj[span, :], NT)
            folded = []
            for t in range(2):
                acc = jnp.zeros((8, cn), f32)
                for o in range(owners):
                    for k2 in range(2):
                        r0 = o * 32 + t * 16 + k2 * 8
                        acc = jnp.where(sm == o * 4 + 2 * k2, dense[r0 : r0 + 8], acc)
                folded.append(acc + roll4(acc))
            mine[g, :, span] = jnp.where(low8, folded[0], folded[1])
            return carry

        lax.fori_loop(0, CHUNKS, score_chunk, 0)
        ssend[g] = jnp.concatenate([mine[g, :, :half_rows], mine[g, :, half_rows:]], axis=0).astype(bf16)
        s_copy(g).start()

    def soften(g):
        s_copy(g).wait()
        got = srecv[g].astype(f32)
        part = (mine[g] + jnp.concatenate([got[:8], got[8:]], axis=1)) * scale
        turned = roll4(part)
        low = lax.broadcasted_iota(i32, (8, rows), 0) < 4
        sm = slotm_ref[...]
        for t in range(2):
            gt = 2 * g + t
            s = jnp.where(low, part, turned) if t == 0 else jnp.where(low, turned, part)
            top_tok = jnp.zeros((8, rows), f32)
            for c in range(2 * owners):
                live = sm == 2 * c
                top = jnp.max(jnp.where(live, s, LOW), axis=1, keepdims=True)
                tops[c, gt] = jnp.broadcast_to(top, (8, 128))
                top_tok = jnp.where(live, top, top_tok)
            p_scr[gt] = jnp.exp(s - top_tok - roll4(top_tok))

    for g in range(4):
        scores(g)
        if g:
            soften(g - 1)
    soften(3)

    def a_copies(o, so):
        return [
            remote(asend.at[o * 2 + t], arecv.at[so * 2 + tp], as_sem.at[o * 2 + t], ar_sem.at[so * 2 + tp], o, t)
            for t in range(2)
        ]

    def t_copy(o, so):
        return remote(tsend.at[o], trecv.at[so], ts_sem.at[o], tr_sem.at[so], o, tp)

    def share(ctx):
        sm = slotm_ref[...]
        tot = []
        for d in range(2):
            for gt in range(8):
                p = p_scr[gt]
                tiles = [jnp.where(sm == ctx * 8 + d * 4 + 2 * k2, p, 0.0) for k2 in range(2)]
                both = jnp.concatenate(tiles, axis=0)
                tot.append(jnp.sum(both, axis=1, keepdims=True))
                r0 = d * 128 + gt * 16
                pblk[r0 : r0 + 16, :] = both.astype(bf16)
        u = dot(pblk[...], proj[...]).astype(bf16)
        stats = [jnp.full((16, 128), LOW, f32) for _ in range(2)]
        for g in range(4):
            rows_g = jnp.concatenate([u[d * 128 + g * 32 : d * 128 + (g + 1) * 32] for d in range(2)], axis=0)
            a = dot(rows_g, bbuf[1, g].reshape(HD, 512), NT)
            for d in range(2):
                o = ctx * 2 + d
                lse = []
                for t in range(2):
                    l = tot[d * 8 + 2 * g + t]
                    inv = 1.0 / jnp.where(l > 0.0, l, 1.0)
                    r0 = d * 32 + t * 16
                    asend[o * 2 + t, :, g * HD : (g + 1) * HD] = (a[r0 : r0 + 16] * inv).astype(bf16)
                    top = jnp.concatenate([tops[2 * o, 2 * g + t], tops[2 * o + 1, 2 * g + t]], axis=0)
                    lse.append(jnp.where(l > 0.0, top + jnp.log(jnp.where(l > 0.0, l, 1.0)), LOW))
                stats[d] = jnp.where(lane_g == g, jnp.where(tp == 0, lse[0], lse[1]), stats[d])
        for d in range(2):
            tsend[ctx * 2 + d] = jnp.where(low_lane, stats[d][:8], stats[d][8:])

    my_ctx = lax.axis_index("ctx")

    def send_all(o):
        for cp in a_copies(o, me):
            cp.start()
        t_copy(o, me).start()

    def share_send(i, carry):
        c = lax.rem(my_ctx + i, owners // 2)
        share(c)
        for d in range(2):
            send_all(c * 2 + d)
        return carry

    lax.fori_loop(1, owners // 2, share_send, 0)
    share(my_ctx)
    send_all(sib)
    pair = remote(
        asend.at[me * 2 + oth], arecv.at[me * 2 + tp], as_sem.at[me * 2 + oth], ar_sem.at[me * 2 + tp], me, oth
    )
    pair.start()
    arecv[me * 2 + tp] = asend[me * 2 + tp]
    trecv[me] = tsend[me]

    def share_wait(i, carry):
        o = lax.rem(me + i, owners)
        for cp in a_copies(o, me):
            cp.wait_send()
        t_copy(o, me).wait_send()
        for t in range(2):
            remote(
                asend.at[o * 2 + t], arecv.at[o * 2 + t], as_sem.at[o * 2 + t], ar_sem.at[o * 2 + t], o, t
            ).wait_recv()
        t_copy(o, o).wait_recv()
        return carry

    lax.fori_loop(1, owners, share_wait, 0)
    pair.wait_send()
    remote(
        asend.at[me * 2 + oth], arecv.at[me * 2 + oth], as_sem.at[me * 2 + oth], ar_sem.at[me * 2 + oth], me, oth
    ).wait_recv()

    own = jnp.where(low_lane, own[:8], own[8:])
    best = own
    for s in range(owners):
        best = jnp.maximum(best, trecv[s])
    own_w = jnp.exp(own - best)
    denom = own_w
    lifts = []
    for s in range(owners):
        lifts.append(jnp.exp(trecv[s] - best))
        denom = denom + lifts[-1]
    inv = 1.0 / denom

    def spread(x, g):
        return jnp.concatenate([x[:, 32 * g : 32 * g + 1], x[:, 32 * g + 16 : 32 * g + 17]], axis=0)

    row_j = lax.rem(lax.broadcasted_iota(i32, (16, 1), 0), 4)
    fold = jnp.where(
        lax.broadcasted_iota(i32, (16, 16), 1) // 4 == lax.rem(lax.broadcasted_iota(i32, (16, 16), 0), 4), 1.0, 0.0
    ).astype(bf16)
    for g in range(4):
        cols = slice(g * HD, (g + 1) * HD)
        att = spread(own_w, g) * fresh[:, 512 + g * HD : 512 + (g + 1) * HD]
        for s in range(owners):
            both = arecv[2 * s, :, cols].astype(f32) + arecv[2 * s + 1, :, cols].astype(f32)
            att = att + spread(lifts[s], g) * both
        att = att * spread(inv, g)
        for j in range(4):
            pick = jnp.where(row_j == j, att, 0.0).astype(bf16)
            x16[:, j * 512 + g * HD : j * 512 + (g + 1) * HD] = dot(fold, pick).astype(bf16)

    o_copy = remote(osend, orecv, o_sem.at[0], o_sem.at[1], me, oth)
    quarter = half_cols // 2
    lowq = lax.broadcasted_iota(i32, (8, 256), 0) < 4
    for h in range(2):
        w_copies[h].wait()

        def column_tile(j, carry, h=h):
            left = pl.ds(pl.multiple_of(j * 256, 256), 256)
            right = pl.ds(pl.multiple_of(quarter + j * 256, 256), 256)
            a = dot(x16[...], w[h, :, left])
            b = dot(x16[...], w[h, :, right])
            picked = jnp.where(lowq, a[:8], b[:8])
            if h == 0:
                osend[:, left] = picked
            else:
                outf[:, left] = picked
            return carry

        lax.fori_loop(0, quarter // 256, column_tile, 0)
        if h == 0:
            o_copy.start()
    o_copy.wait()
    total = outf[...] + orecv[...]
    out_ref[:, :quarter] = total[:4].astype(bf16)
    out_ref[:, quarter:] = roll4(total)[:4].astype(bf16)


def fused(kv_rows, basis, out_weight, queries, new_kv, owner, req_start):
    f32, bf16 = jnp.float32, jnp.bfloat16
    owners = lax.axis_size("ctx") * lax.axis_size("dp")
    rows = kv_rows.shape[0]
    half_cols = out_weight.shape[1] // 2
    dma = pltpu.SemaphoreType.DMA
    vm = pl.BlockSpec(memory_space=pltpu.VMEM)
    hbm = pl.BlockSpec(memory_space=pl.ANY)
    out = pl.pallas_call(
        handoff_kernel,
        out_shape=jax.ShapeDtypeStruct((4, half_cols), bf16),
        in_specs=[vm, vm, vm, vm, vm, hbm, hbm],
        out_specs=vm,
        scratch_shapes=[
            pltpu.VMEM((rows, 512), bf16),
            pltpu.VMEM((2, out_weight.shape[0], half_cols), bf16),
            pltpu.VMEM((16, 512), bf16),
            pltpu.VMEM((owners, 2, 16, 512), bf16),
            pltpu.VMEM((2, 4, 2, HD // 2, 512), bf16),
            pltpu.VMEM((rows, 512), bf16),
            pltpu.VMEM((8, rows), jnp.int32),
            pltpu.VMEM((4, 8, rows), f32),
            pltpu.VMEM((4, 16, rows // 2), bf16),
            pltpu.VMEM((4, 16, rows // 2), bf16),
            pltpu.VMEM((8, 8, rows), f32),
            pltpu.VMEM((2 * owners, 8, 8, 128), f32),
            pltpu.VMEM((256, rows), bf16),
            pltpu.VMEM((2 * owners, 16, 512), bf16),
            pltpu.VMEM((2 * owners, 16, 512), bf16),
            pltpu.VMEM((owners, 8, 128), f32),
            pltpu.VMEM((owners, 8, 128), f32),
            pltpu.VMEM((16, out_weight.shape[0]), bf16),
            pltpu.VMEM((8, half_cols // 2), f32),
            pltpu.VMEM((8, half_cols // 2), f32),
            pltpu.VMEM((8, half_cols // 2), f32),
            dma((3,)), dma((2,)), dma((owners,)), dma((owners,)), dma((16,)),
            dma((4,)), dma((4,)),
            dma((2 * owners,)), dma((2 * owners,)), dma((owners,)), dma((owners,)), dma((2,)),
        ],
        compiler_params=pltpu.CompilerParams(
            collective_id=0, has_side_effects=True, vmem_limit_bytes=56 * 1024 * 1024
        ),
    )(
        owner.reshape(1, -1), req_start, queries, new_kv, basis, kv_rows, out_weight,
    )
    return out


def on_device(kv_rows, basis, out_weight, queries, new_kv, owner, req_start):
    args = (kv_rows, basis, out_weight, queries, new_kv, owner, req_start)
    if queries.shape == (4, 4, 512) and lax.axis_size("tp") == 2 and lax.axis_size("dp") == 2:
        return fused(*args)
    return by_collectives(*args)


def solution(mesh):
    return jax.shard_map(
        on_device,
        mesh=mesh,
        in_specs=(
            P(("groups", "ctx", "dp"), "tp"),
            P("tp", None),
            P("tp", None),
            P(("groups", "ctx", "dp"), "tp", None),
            P(("groups", "ctx", "dp"), None),
            P("groups"),
            P(("groups", "ctx", "dp"), None),
        ),
        out_specs=P(("groups", "ctx", "dp"), "tp"),
        check_vma=False,
    )
```

```python
import math

import jax
import jax.numpy as jnp
from jax import lax
from jax.experimental import pallas as pl
from jax.experimental.pallas import tpu as pltpu
from jax.sharding import PartitionSpec as P

HD = 128


def token_slots(owner, req_start, row_count, slot_own):
    starts = req_start[0]
    req_count = starts.shape[0]
    row_ids = jnp.arange(row_count, dtype=jnp.int32)
    req_ids = jnp.arange(req_count, dtype=jnp.int32)
    inside = (starts[None, :] <= row_ids[:, None]).astype(jnp.int32)
    request_of = jnp.sum(inside, axis=1) - 1
    picked = (request_of[:, None] == req_ids[None, :]).astype(jnp.int32)
    earlier = (owner[:, None] == owner[None, :]) & (req_ids[None, :] < req_ids[:, None])
    slot_of = owner * slot_own + jnp.sum(earlier.astype(jnp.int32), axis=1)
    return jnp.sum(picked * slot_of[None, :], axis=1)


def by_collectives(kv_rows, basis, out_weight, queries, new_kv, owner, req_start):
    owners = lax.axis_size("ctx") * lax.axis_size("dp")
    rows, feat = kv_rows.shape
    own_slots, local_j, half = queries.shape
    groups = half // HD
    f32, bf16 = jnp.float32, jnp.bfloat16
    scale = 1.0 / math.sqrt(HD)
    whole_basis = lax.all_gather(basis, "tp", axis=0, tiled=True)
    rank = basis.shape[1]
    basis_k = whole_basis[:half].reshape(groups, HD, rank)
    basis_v = whole_basis[half:].reshape(groups, HD, rank)
    q_all = lax.all_gather(queries, ("ctx", "dp"), axis=0, tiled=True)
    q_all = lax.all_gather(q_all, "tp", axis=1, tiled=True)
    slots, heads = q_all.shape[:2]
    q4 = q_all.reshape(slots, heads, groups, HD)
    q_rank = jnp.einsum("rjgd,gdl->grjl", q4, basis_k, preferred_element_type=f32).astype(bf16)
    q_feat = jnp.einsum("grjl,fl->grjf", q_rank, basis, preferred_element_type=f32).astype(bf16)
    slot = token_slots(owner, req_start, rows, own_slots)
    slot_ids = jnp.arange(slots, dtype=jnp.int32)
    live = slot_ids[:, None] == slot[None, :]
    dense = jnp.einsum("grjf,nf->grjn", q_feat, kv_rows, preferred_element_type=f32)
    part = jnp.sum(jnp.where(live[None, :, None, :], dense, 0.0), axis=1)
    score = lax.psum(part, "tp") * scale
    top = jnp.max(jnp.where(live[None, :, None, :], score[:, None], -1e30), axis=3)
    top_tok = jnp.sum(jnp.where(live[None, :, None, :], top[..., None], 0.0), axis=1)
    p = jnp.exp(score - top_tok)
    spread = jnp.where(live[None, :, None, :], p[:, None], 0.0)
    total = jnp.sum(spread, axis=3)
    mixed = jnp.einsum("grjn,nf->grjf", spread.astype(bf16), kv_rows, preferred_element_type=f32)
    mixed = jnp.einsum("grjf,fl->grjl", mixed.astype(bf16), basis, preferred_element_type=f32)
    mixed = jnp.einsum("grjl,gdl->jrgd", mixed.astype(bf16), basis_v, preferred_element_type=f32)
    mixed = lax.psum_scatter(mixed.astype(bf16), "tp", scatter_dimension=0, tiled=True)
    first_j = lax.axis_index("tp") * local_j
    stats = jnp.stack([top, total]).transpose(3, 2, 1, 0)
    stats = lax.dynamic_slice_in_dim(stats, first_j, local_j, axis=0)
    mixed = lax.all_to_all(
        mixed.reshape(local_j, owners, own_slots, groups, HD), ("ctx", "dp"), 1, 1, tiled=True
    ).astype(f32)
    stats = lax.all_to_all(
        stats.reshape(local_j, owners, own_slots, groups, 2), ("ctx", "dp"), 1, 1, tiled=True
    )
    q_own = queries.reshape(own_slots, local_j, groups, HD)
    new_keys = new_kv[:, :half].reshape(own_slots, groups, HD)
    new_values = new_kv[:, half:].reshape(own_slots, groups, HD)
    own = jnp.einsum("rjgd,rgd->jrg", q_own, new_keys, preferred_element_type=f32) * scale
    tops, totals = stats[..., 0], stats[..., 1]
    best = jnp.maximum(jnp.max(tops, axis=1), own)
    lift = jnp.exp(tops - best[:, None])
    own_w = jnp.exp(own - best)
    denom = jnp.sum(lift * totals, axis=1) + own_w
    att = jnp.sum(lift[..., None] * mixed, axis=1)
    att = att + own_w[..., None] * new_values.astype(f32)[None]
    att = (att / denom[..., None]).astype(bf16)
    att = att.transpose(1, 0, 2, 3).reshape(own_slots, local_j * half)
    out = jnp.dot(att, out_weight, preferred_element_type=f32)
    return lax.psum_scatter(out.astype(bf16), "tp", scatter_dimension=1, tiled=True)

NT = (((1,), (1,)), ((), ()))
NN = (((1,), (0,)), ((), ()))
LOW = -1e30
CHUNKS = 4


def dot(a, b, dims=NN):
    return lax.dot_general(a, b, dims, preferred_element_type=jnp.float32)


def roll4(x):
    return pltpu.roll(x, 4, 0)


def handoff_kernel(
    owner_ref, start_ref, q3_ref, new_ref, basis_ref, kv_hbm, w_hbm, out_ref,
    kv, w, q_ref, qbuf, bbuf, proj, slotm_ref, mine, ssend, srecv, p_scr, tops,
    pblk, asend, arecv, tsend, trecv, x16, osend, orecv, outf,
    loc_sem, q1_sem, qs_sem, qr_sem, b_sem, s_sem, r_sem, as_sem, ar_sem, ts_sem, tr_sem, o_sem,
):
    f32, bf16, i32 = jnp.float32, jnp.bfloat16, jnp.int32
    owners = qbuf.shape[0]
    slots = 4 * owners
    rows = kv.shape[0]
    cn = rows // CHUNKS
    scale = 1.0 / math.sqrt(HD)
    dp, tp = lax.axis_index("dp"), lax.axis_index("tp")
    me = lax.axis_index("ctx") * 2 + dp
    oth = 1 - tp
    half_cols = w.shape[2]

    def at(o, t):
        return {"ctx": o // 2, "dp": lax.rem(o, 2), "tp": t}

    def remote(src, dst, ssem, rsem, o, t):
        return pltpu.make_async_remote_copy(
            src_ref=src, dst_ref=dst, send_sem=ssem, recv_sem=rsem,
            device_id=at(o, t), device_id_type=pl.DeviceIdType.MESH,
        )

    kv_copy = pltpu.make_async_copy(kv_hbm, kv, loc_sem.at[0])
    kv_copy.start()
    w_copies = []
    for h, side in enumerate((oth, tp)):
        cols = pl.ds(pl.multiple_of(side * half_cols, half_cols), half_cols)
        w_copies.append(pltpu.make_async_copy(w_hbm.at[:, cols], w.at[h], loc_sem.at[1 + h]))
        w_copies[-1].start()

    q_ref[...] = jnp.concatenate([q3_ref[k].astype(f32) for k in range(4)], axis=0).astype(bf16)
    barrier = pltpu.get_barrier_semaphore()

    def greet(i, c):
        o = lax.rem(me + i, owners)
        for t in range(2):
            pl.semaphore_signal(barrier, inc=1, device_id=at(o, t), device_id_type=pl.DeviceIdType.MESH)
        return c

    lax.fori_loop(1, owners, greet, 0)
    pl.semaphore_signal(barrier, inc=1, device_id=at(me, oth), device_id_type=pl.DeviceIdType.MESH)
    pl.semaphore_wait(barrier, 2 * owners - 1)

    q1 = remote(q_ref, qbuf.at[me, tp], q1_sem.at[0], q1_sem.at[1], me, oth)
    q1.start()
    sib = 2 * lax.axis_index("ctx") + 1 - dp
    hb = bbuf.shape[3]

    def b_first(g):
        return remote(
            basis_ref.at[pl.ds(pl.multiple_of(g * HD + dp * hb, hb), hb)], bbuf.at[tp, g, dp],
            b_sem.at[g], b_sem.at[4 + g], me, oth,
        )

    def b_second(g):
        return remote(bbuf.at[oth, g, dp], bbuf.at[oth, g, dp], b_sem.at[8 + g], b_sem.at[12 + g], sib, tp)

    for g in range(2):
        b_first(g).start()
    qbuf[me, tp] = q_ref[...]
    q1.wait()

    def q_copy(o, src):
        return remote(qbuf.at[me], qbuf.at[src], qs_sem.at[o], qr_sem.at[src], o, tp)

    def q_start(i, c):
        q_copy(lax.rem(me + i, owners), me).start()
        return c

    lax.fori_loop(1, owners, q_start, 0)

    for g in range(4):
        for d in range(2):
            r0 = g * HD + d * hb
            bbuf[tp, g, d] = basis_ref[r0 : r0 + hb]
    req = owner_ref.shape[1]
    ri = lax.broadcasted_iota(i32, (req, req), 0)
    ci = lax.broadcasted_iota(i32, (req, req), 1)

    def column(row, shift=0):
        return jnp.sum(jnp.where(ci == ri + shift, jnp.broadcast_to(row, (req, req)), 0), axis=1, keepdims=True)

    own_row = owner_ref[...]
    own_col = column(own_row)
    same = (own_row == own_col) & (ci < ri)
    slot_col = own_col * 4 + jnp.sum(jnp.where(same, 1, 0), axis=1, keepdims=True)
    first = column(start_ref[...])
    rc = lax.broadcasted_iota(i32, (req, 1), 0)
    last = column(start_ref[...], 1) + jnp.where(rc == req - 1, rows, 0)
    tok = lax.broadcasted_iota(i32, (req, rows), 1)
    slot = jnp.sum(jnp.where((tok >= first) & (tok < last), slot_col, 0), axis=0, keepdims=True)
    slotm_ref[...] = jnp.broadcast_to(slot, (8, rows)) - lax.broadcasted_iota(i32, (8, rows), 0) // 4

    low_lane = lax.rem(lax.broadcasted_iota(i32, (8, 128), 1), 32) < 16
    lane_g = lax.broadcasted_iota(i32, (16, 128), 1) // 32
    row_k = lax.broadcasted_iota(i32, (16, 1), 0) // 4
    fresh = jnp.zeros((16, 1024), f32)
    for k in range(4):
        fresh = jnp.where(row_k == k, new_ref[k : k + 1, :].astype(f32), fresh)
    qk = q_ref[...].astype(f32) * fresh[:, :512]
    own = jnp.zeros((16, 128), f32)
    for g in range(4):
        s = jnp.sum(qk[:, g * HD : (g + 1) * HD], axis=1, keepdims=True) * scale
        own = jnp.where(lane_g == g, s, own)

    kv_copy.wait()

    def project(c, carry):
        span = pl.ds(pl.multiple_of(c * cn, cn), cn)
        proj[span, :] = dot(kv[span, :], basis_ref[...]).astype(bf16)
        return carry

    lax.fori_loop(0, CHUNKS, project, 0)

    def pass_on(g):
        b_first(g).wait()
        b_second(g).start()
        if g < 2:
            b_first(g + 2).start()

    pass_on(0)
    pass_on(1)

    def q_wait(i, c):
        o = lax.rem(me + i, owners)
        cp = q_copy(o, o)
        cp.wait_recv()
        q_copy(o, me).wait_send()
        return c

    lax.fori_loop(1, owners, q_wait, 0)
    q_rows = qbuf[...].reshape(slots * 8, 512)
    low8 = lax.broadcasted_iota(i32, (8, cn), 0) < 4
    half_rows = rows // 2

    def s_copy(g):
        return remote(ssend.at[g], srecv.at[g], s_sem.at[g], r_sem.at[g], me, oth)

    def scores(g):
        b_second(g).wait()
        qg = dot(q_rows[:, g * HD : (g + 1) * HD], bbuf[0, g].reshape(HD, 512)).astype(bf16)

        def score_chunk(c, carry):
            span = pl.ds(pl.multiple_of(c * cn, cn), cn)
            sm = slotm_ref[:, span]
            dense = dot(qg, proj[span, :], NT)
            folded = []
            for t in range(2):
                acc = jnp.zeros((8, cn), f32)
                for o in range(owners):
                    for k2 in range(2):
                        r0 = o * 32 + t * 16 + k2 * 8
                        acc = jnp.where(sm == o * 4 + 2 * k2, dense[r0 : r0 + 8], acc)
                folded.append(acc + roll4(acc))
            mine[g, :, span] = jnp.where(low8, folded[0], folded[1])
            return carry

        lax.fori_loop(0, CHUNKS, score_chunk, 0)
        ssend[g] = jnp.concatenate([mine[g, :, :half_rows], mine[g, :, half_rows:]], axis=0).astype(bf16)
        s_copy(g).start()

    def soften(g):
        s_copy(g).wait()
        got = srecv[g].astype(f32)
        part = (mine[g] + jnp.concatenate([got[:8], got[8:]], axis=1)) * scale
        turned = roll4(part)
        low = lax.broadcasted_iota(i32, (8, rows), 0) < 4
        sm = slotm_ref[...]
        for t in range(2):
            gt = 2 * g + t
            s = jnp.where(low, part, turned) if t == 0 else jnp.where(low, turned, part)
            top_tok = jnp.zeros((8, rows), f32)
            for c in range(2 * owners):
                live = sm == 2 * c
                top = jnp.max(jnp.where(live, s, LOW), axis=1, keepdims=True)
                tops[c, gt] = jnp.broadcast_to(top, (8, 128))
                top_tok = jnp.where(live, top, top_tok)
            p_scr[gt] = jnp.exp(s - top_tok - roll4(top_tok))

    scores(0)
    pass_on(2)
    scores(1)
    pass_on(3)
    soften(0)
    scores(2)
    soften(1)
    scores(3)
    soften(2)
    soften(3)

    def a_copies(o, so):
        return [
            remote(asend.at[o * 2 + t], arecv.at[so * 2 + tp], as_sem.at[o * 2 + t], ar_sem.at[so * 2 + tp], o, t)
            for t in range(2)
        ]

    def t_copy(o, so):
        return remote(tsend.at[o], trecv.at[so], ts_sem.at[o], tr_sem.at[so], o, tp)

    def share(ctx):
        sm = slotm_ref[...]
        tot = []
        for d in range(2):
            for gt in range(8):
                p = p_scr[gt]
                tiles = [jnp.where(sm == ctx * 8 + d * 4 + 2 * k2, p, 0.0) for k2 in range(2)]
                both = jnp.concatenate(tiles, axis=0)
                tot.append(jnp.sum(both, axis=1, keepdims=True))
                r0 = d * 128 + gt * 16
                pblk[r0 : r0 + 16, :] = both.astype(bf16)
        u = dot(pblk[...], proj[...]).astype(bf16)
        stats = [jnp.full((16, 128), LOW, f32) for _ in range(2)]
        for g in range(4):
            rows_g = jnp.concatenate([u[d * 128 + g * 32 : d * 128 + (g + 1) * 32] for d in range(2)], axis=0)
            a = dot(rows_g, bbuf[1, g].reshape(HD, 512), NT)
            for d in range(2):
                o = ctx * 2 + d
                lse = []
                for t in range(2):
                    l = tot[d * 8 + 2 * g + t]
                    inv = 1.0 / jnp.where(l > 0.0, l, 1.0)
                    r0 = d * 32 + t * 16
                    asend[o * 2 + t, :, g * HD : (g + 1) * HD] = (a[r0 : r0 + 16] * inv).astype(bf16)
                    top = jnp.concatenate([tops[2 * o, 2 * g + t], tops[2 * o + 1, 2 * g + t]], axis=0)
                    lse.append(jnp.where(l > 0.0, top + jnp.log(jnp.where(l > 0.0, l, 1.0)), LOW))
                stats[d] = jnp.where(lane_g == g, jnp.where(tp == 0, lse[0], lse[1]), stats[d])
        for d in range(2):
            tsend[ctx * 2 + d] = jnp.where(low_lane, stats[d][:8], stats[d][8:])

    my_ctx = lax.axis_index("ctx")

    def send_all(o):
        for cp in a_copies(o, me):
            cp.start()
        t_copy(o, me).start()

    def share_send(i, carry):
        c = lax.rem(my_ctx + i, owners // 2)
        share(c)
        for d in range(2):
            send_all(c * 2 + d)
        return carry

    lax.fori_loop(1, owners // 2, share_send, 0)
    share(my_ctx)
    send_all(sib)
    pair = remote(
        asend.at[me * 2 + oth], arecv.at[me * 2 + tp], as_sem.at[me * 2 + oth], ar_sem.at[me * 2 + tp], me, oth
    )
    pair.start()
    arecv[me * 2 + tp] = asend[me * 2 + tp]
    trecv[me] = tsend[me]

    def share_wait(i, carry):
        o = lax.rem(me + i, owners)
        for cp in a_copies(o, me):
            cp.wait_send()
        t_copy(o, me).wait_send()
        for t in range(2):
            remote(
                asend.at[o * 2 + t], arecv.at[o * 2 + t], as_sem.at[o * 2 + t], ar_sem.at[o * 2 + t], o, t
            ).wait_recv()
        t_copy(o, o).wait_recv()
        return carry

    lax.fori_loop(1, owners, share_wait, 0)
    pair.wait_send()
    remote(
        asend.at[me * 2 + oth], arecv.at[me * 2 + oth], as_sem.at[me * 2 + oth], ar_sem.at[me * 2 + oth], me, oth
    ).wait_recv()

    own = jnp.where(low_lane, own[:8], own[8:])
    best = own
    for s in range(owners):
        best = jnp.maximum(best, trecv[s])
    own_w = jnp.exp(own - best)
    denom = own_w
    lifts = []
    for s in range(owners):
        lifts.append(jnp.exp(trecv[s] - best))
        denom = denom + lifts[-1]
    inv = 1.0 / denom

    def spread(x, g):
        return jnp.concatenate([x[:, 32 * g : 32 * g + 1], x[:, 32 * g + 16 : 32 * g + 17]], axis=0)

    row_j = lax.rem(lax.broadcasted_iota(i32, (16, 1), 0), 4)
    fold = jnp.where(
        lax.broadcasted_iota(i32, (16, 16), 1) // 4 == lax.rem(lax.broadcasted_iota(i32, (16, 16), 0), 4), 1.0, 0.0
    ).astype(bf16)
    for g in range(4):
        cols = slice(g * HD, (g + 1) * HD)
        att = spread(own_w, g) * fresh[:, 512 + g * HD : 512 + (g + 1) * HD]
        for s in range(owners):
            both = arecv[2 * s, :, cols].astype(f32) + arecv[2 * s + 1, :, cols].astype(f32)
            att = att + spread(lifts[s], g) * both
        att = att * spread(inv, g)
        for j in range(4):
            pick = jnp.where(row_j == j, att, 0.0).astype(bf16)
            x16[:, j * 512 + g * HD : j * 512 + (g + 1) * HD] = dot(fold, pick).astype(bf16)

    o_copy = remote(osend, orecv, o_sem.at[0], o_sem.at[1], me, oth)
    quarter = half_cols // 2
    lowq = lax.broadcasted_iota(i32, (8, 256), 0) < 4
    for h in range(2):
        w_copies[h].wait()

        def column_tile(j, carry, h=h):
            left = pl.ds(pl.multiple_of(j * 256, 256), 256)
            right = pl.ds(pl.multiple_of(quarter + j * 256, 256), 256)
            a = dot(x16[...], w[h, :, left])
            b = dot(x16[...], w[h, :, right])
            picked = jnp.where(lowq, a[:8], b[:8])
            if h == 0:
                osend[:, left] = picked
            else:
                outf[:, left] = picked
            return carry

        lax.fori_loop(0, quarter // 256, column_tile, 0)
        if h == 0:
            o_copy.start()
    o_copy.wait()
    total = outf[...] + orecv[...]
    out_ref[:, :quarter] = total[:4].astype(bf16)
    out_ref[:, quarter:] = roll4(total)[:4].astype(bf16)


def fused(kv_rows, basis, out_weight, queries, new_kv, owner, req_start):
    f32, bf16 = jnp.float32, jnp.bfloat16
    owners = lax.axis_size("ctx") * lax.axis_size("dp")
    rows = kv_rows.shape[0]
    half_cols = out_weight.shape[1] // 2
    dma = pltpu.SemaphoreType.DMA
    vm = pl.BlockSpec(memory_space=pltpu.VMEM)
    hbm = pl.BlockSpec(memory_space=pl.ANY)
    out = pl.pallas_call(
        handoff_kernel,
        out_shape=jax.ShapeDtypeStruct((4, half_cols), bf16),
        in_specs=[vm, vm, vm, vm, vm, hbm, hbm],
        out_specs=vm,
        scratch_shapes=[
            pltpu.VMEM((rows, 512), bf16),
            pltpu.VMEM((2, out_weight.shape[0], half_cols), bf16),
            pltpu.VMEM((16, 512), bf16),
            pltpu.VMEM((owners, 2, 16, 512), bf16),
            pltpu.VMEM((2, 4, 2, HD // 2, 512), bf16),
            pltpu.VMEM((rows, 512), bf16),
            pltpu.VMEM((8, rows), jnp.int32),
            pltpu.VMEM((4, 8, rows), f32),
            pltpu.VMEM((4, 16, rows // 2), bf16),
            pltpu.VMEM((4, 16, rows // 2), bf16),
            pltpu.VMEM((8, 8, rows), f32),
            pltpu.VMEM((2 * owners, 8, 8, 128), f32),
            pltpu.VMEM((256, rows), bf16),
            pltpu.VMEM((2 * owners, 16, 512), bf16),
            pltpu.VMEM((2 * owners, 16, 512), bf16),
            pltpu.VMEM((owners, 8, 128), f32),
            pltpu.VMEM((owners, 8, 128), f32),
            pltpu.VMEM((16, out_weight.shape[0]), bf16),
            pltpu.VMEM((8, half_cols // 2), f32),
            pltpu.VMEM((8, half_cols // 2), f32),
            pltpu.VMEM((8, half_cols // 2), f32),
            dma((3,)), dma((2,)), dma((owners,)), dma((owners,)), dma((16,)),
            dma((4,)), dma((4,)),
            dma((2 * owners,)), dma((2 * owners,)), dma((owners,)), dma((owners,)), dma((2,)),
        ],
        compiler_params=pltpu.CompilerParams(
            collective_id=0, has_side_effects=True, vmem_limit_bytes=56 * 1024 * 1024
        ),
    )(
        owner.reshape(1, -1), req_start, queries, new_kv, basis, kv_rows, out_weight,
    )
    return out


def on_device(kv_rows, basis, out_weight, queries, new_kv, owner, req_start):
    args = (kv_rows, basis, out_weight, queries, new_kv, owner, req_start)
    if queries.shape == (4, 4, 512) and lax.axis_size("tp") == 2 and lax.axis_size("dp") == 2:
        return fused(*args)
    return by_collectives(*args)


def solution(mesh):
    return jax.shard_map(
        on_device,
        mesh=mesh,
        in_specs=(
            P(("groups", "ctx", "dp"), "tp"),
            P("tp", None),
            P("tp", None),
            P(("groups", "ctx", "dp"), "tp", None),
            P(("groups", "ctx", "dp"), None),
            P("groups"),
            P(("groups", "ctx", "dp"), None),
        ),
        out_specs=P(("groups", "ctx", "dp"), "tp"),
        check_vma=False,
    )
```
